512 devices in a mesh: team: 16 (over y_lo, x, core), row: 32 (over y_hi, z).
Axes of the slice: x: 4, y: 4 (y_hi: 2, y_lo: 2; y = y_hi * 2 + y_lo), z: 16, core: 2. Of those that a mesh axis runs over, the one named last changes fastest.
Arguments:
- features: bfloat16 [16384, 128], P('row'), may hold values from -6 to 6
- tile_vals: bfloat16 [32, 16, 128, 128, 128], P('row', 'team'), may hold values from 0 to 1
- tile_row: int32 [32, 16, 128], P('row', 'team'), may hold values from 0 to 3
- tile_col: int32 [32, 16, 128], P('row', 'team'), may hold values from 0 to 127, as said below
- tile_count: int32 [32, 16], P('row', 'team'), may hold values from 1 to 128, as said below
- weight: bfloat16 [128, 256], replicated, may hold values from -0.5 to 0.5
- bias: float32 [256], replicated, may hold values from -3 to 3
- cotangent: bfloat16 [16384, 256], P('row'), may hold values from -0.125 to 0.125
Outputs:
- activated: bfloat16 [16384, 256], P('row')
- weight_grad: float32 [128, 256], replicated
- bias_grad: float32 [256], replicated
The draws below stay inside these ranges and needn't reach their ends.
Inputs may be any that keep to these rules, and one draw needn't show every extreme that they name: The owner index tile_col // 4 equals t + k * 16 for the device's team index t and some k < 2, in every slot. A device's live slots are its first tile_count slots; some device has all 128 live in every draw.
All inputs are finite; a program needn't handle non-finite values.
Results may differ from the reference program's by a relative error of at most 0.0075.
Values may be sent and summed in bfloat16 or wider, within the bound.
A program may use at most 64 MiB of HBM per device.

```python
import jax
import jax.numpy as jnp
from jax import lax

FEAT = 128
HIDDEN_SIZE = 256
TILE = 128
BLK_DEV = 4
SLOTS = 128
BLOCKS = 128
NODES = 16384
OWNERS = 2
N_TEAM = 16
N_ROW = 32


def draw_tile_col(key, part):
    key = jax.random.fold_in(key, 11)
    key_owner, key_block = jax.random.split(key)
    owner_pick = jax.random.randint(key_owner, (N_ROW, N_TEAM, SLOTS), 0, OWNERS)
    block_pick = jax.random.randint(key_block, (N_ROW, N_TEAM, SLOTS), 0, BLK_DEV)
    team_line = lax.broadcasted_iota(jnp.int32, (N_ROW, N_TEAM, SLOTS), 1)
    return ((team_line + owner_pick * N_TEAM) * BLK_DEV + block_pick).astype(jnp.int32)


def draw_tile_count(key, part):
    key = jax.random.fold_in(key, 12)
    key_level, key_place = jax.random.split(key)
    levels = jax.random.randint(key_level, (N_ROW * N_TEAM,), 0, SLOTS + 1)
    counts = jnp.maximum(1, levels * levels // SLOTS)
    chosen = jax.random.randint(key_place, (), 0, N_ROW * N_TEAM)
    counts = jnp.where(jnp.arange(N_ROW * N_TEAM) == chosen, SLOTS, counts)
    return counts.reshape(N_ROW, N_TEAM).astype(jnp.int32)


def plant(entries, key, smallest, high):
    longest = entries.shape.index(max(entries.shape))
    spots = []
    for shift in (0, 1):
        where = [jax.random.randint(jax.random.fold_in(key, axis), (), 0, length) for axis, length in enumerate(entries.shape)]
        where[longest] = (where[longest] + shift) % entries.shape[longest]
        spots.append(tuple(where))
    return entries.at[spots[0]].set(smallest).at[spots[1]].set(high)


def shard_levels(key, extent, shards, low, high):
    factor_of, own = 1.0, jax.random.fold_in(key, 6)
    for position, blocks in shards:
        steps = jnp.exp(jax.random.uniform(jax.random.fold_in(own, position), (blocks,), jnp.float32, low / len(shards), high / len(shards)))
        factor_of = factor_of * jnp.repeat(steps, extent[position] // blocks).reshape([-1 if axis == position else 1 for axis in range(len(extent))])
    return factor_of


def gaussian(key, dims, deviation, reach, pieces=(), kind=jnp.bfloat16):
    values = jax.random.normal(key, dims, jnp.float32) * deviation
    if len(pieces) > 0:
        values = shard_levels(key, dims, pieces, -0.22, 0.18) * values
    return jnp.clip(values, min=-reach, max=reach).astype(kind)


def setup_inputs(seed: int = 0) -> dict:
    splits = jax.random.split(jax.random.key(seed), 9)
    features = gaussian(splits[0], (NODES, FEAT), 1.0, 6.0, ((0, 32),))
    tile_vals = jnp.clip(1.0 * jax.random.uniform(splits[1], (N_ROW, N_TEAM, SLOTS, TILE, TILE), jnp.float32) ** shard_levels(splits[1], (N_ROW, N_TEAM, SLOTS, TILE, TILE), ((0, 32), (1, 16)), -0.2, 0.2), 0.0, 1.0).astype(jnp.bfloat16)
    tile_row = plant(jax.random.randint(splits[2], (N_ROW, N_TEAM, SLOTS), 0, BLK_DEV), jax.random.fold_in(splits[2], 1), 0, BLK_DEV - 1).astype(jnp.int32)
    tile_col = draw_tile_col(jax.random.fold_in(splits[8], 71), 0)
    tile_count = draw_tile_count(jax.random.fold_in(splits[8], 71), 0)
    weight = gaussian(splits[5], (FEAT, HIDDEN_SIZE), FEAT ** -0.5, 0.5)
    bias = gaussian(splits[6], (HIDDEN_SIZE,), 0.5, 3.0, (), jnp.float32)
    cotangent = gaussian(splits[7], (NODES, HIDDEN_SIZE), (NODES ** -0.5), 0.125, ((0, 32),))
    return dict(features=features, tile_vals=tile_vals, tile_row=tile_row, tile_col=tile_col, tile_count=tile_count, weight=weight, bias=bias, cotangent=cotangent)


highest = lax.Precision.HIGHEST

def reference(features, tile_vals, tile_row, tile_col, tile_count, weight, bias, cotangent):
    feature_table = features.reshape(BLOCKS, TILE, FEAT).astype(jnp.float32)

    def one_row(row_index):
        adjacency = tile_vals[row_index].reshape(N_TEAM * SLOTS, TILE, TILE).astype(jnp.float32)
        col_slot = tile_col[row_index].reshape(N_TEAM * SLOTS)
        slot_line = jnp.arange(SLOTS, dtype=jnp.int32)
        live_slot = (slot_line[None, :] < tile_count[row_index][:, None]).reshape(N_TEAM * SLOTS)
        selector = tile_row[row_index].reshape(N_TEAM * SLOTS)[:, None] == jnp.arange(BLK_DEV, dtype=jnp.int32)[None, :]
        selector = (selector & live_slot[:, None]).astype(jnp.float32)
        products = jnp.einsum('sij,sjf->sif', adjacency, feature_table[col_slot], precision=highest)
        aggregate = jnp.einsum('sb,sif->bif', selector, products, precision=highest)
        row_sums = lax.optimization_barrier(jnp.sum(adjacency, axis=2))
        degree = 1.0 + jnp.einsum('sb,si->bi', selector, row_sums, precision=highest)
        return (aggregate, degree)
    aggregate, degree = lax.map(one_row, jnp.arange(N_ROW, dtype=jnp.int32))
    aggregate = aggregate.reshape(NODES, FEAT)
    degree = degree.reshape(NODES)
    normed = (aggregate / jnp.sqrt(degree)[:, None]).astype(jnp.bfloat16)
    pre_act = jnp.dot(normed, weight, preferred_element_type=jnp.float32) + bias
    activated = jax.nn.silu(pre_act).astype(jnp.bfloat16)
    gate_value = jax.nn.sigmoid(pre_act)
    delta = (cotangent.astype(jnp.float32) * gate_value * (1.0 + pre_act * (1.0 - gate_value))).astype(jnp.bfloat16)
    weight_grad = lax.dot_general(normed, delta, (((0,), (0,)), ((), ())), preferred_element_type=jnp.float32)
    bias_grad = lax.optimization_barrier(jnp.sum(delta.astype(jnp.float32), axis=0))
    return (activated, weight_grad, bias_grad)
```

```python
import functools

import jax
import jax.numpy as jnp
from jax import lax
from jax.experimental import pallas as pl
from jax.experimental.pallas import tpu as pltpu
from jax.sharding import PartitionSpec as P

MESH = pl.DeviceIdType.MESH
BF16, F32 = jnp.bfloat16, jnp.float32
SIDE = 128
GROUP = 8


def wait_bytes(ref, sem):
    pltpu.make_async_copy(ref, ref, sem).wait()


def kernel(
    T, Z, feat, tiles, trow, tcol, tcount, weight, bias, cot,
    act_out, dw_out, db_out,
    a_vm, zbuf, table, agg, aggs, deg, degs, dgacc, degr, aggr, nbuf, w_vm, b_vm, c_vm, act_vm,
    delta, dwp, piece, pieces_in, full, dw_all,
    tile_sem, w_sem, b_sem, c_sem, a1_send, a1_recv, a2_send, a2_recv, g_send, g_recv, p_send, p_recv,
    n_send, n_recv, d1_send, d1_recv, d2_send, d2_recv, e_send, e_recv, act_sem,
):
    R = 2 * Z
    slots = a_vm.shape[0]
    rows = nbuf.shape[0]
    blocks = rows // SIDE
    PR = rows // T
    r, t = lax.axis_index("row"), lax.axis_index("team")
    k, z = r // Z, r % Z

    def remote(src, dst, ssem, rsem, row, team):
        pltpu.make_async_remote_copy(
            src_ref=src, dst_ref=dst, send_sem=ssem, recv_sem=rsem,
            device_id={"row": row, "team": team}, device_id_type=MESH,
        ).start()

    tile_copy = pltpu.make_async_copy(tiles, a_vm, tile_sem)
    tile_copy.start()
    mine = pl.ds(pl.multiple_of(t * PR, PR), PR)
    pltpu.make_async_copy(feat.at[mine], zbuf.at[z], a1_recv.at[z]).start()
    w_copy = pltpu.make_async_copy(weight, w_vm, w_sem)
    b_copy = pltpu.make_async_copy(bias, b_vm, b_sem)
    c_copy = pltpu.make_async_copy(cot, c_vm, c_sem)
    w_copy.start()
    b_copy.start()
    c_copy.start()

    barrier = pltpu.get_barrier_semaphore()

    @pl.loop(1, R)
    def _(o):
        pl.semaphore_signal(barrier, inc=1, device_id={"row": (r + o) % R, "team": t}, device_id_type=MESH)

    @pl.loop(1, T)
    def _(o):
        u = (t + o) % T
        pl.semaphore_signal(barrier, inc=1, device_id={"row": z, "team": u}, device_id_type=MESH)
        pl.semaphore_signal(barrier, inc=1, device_id={"row": Z + z, "team": u}, device_id_type=MESH)

    pl.semaphore_wait(barrier, R - 1 + 2 * (T - 1))

    def far_first(i):
        d = Z // 2 - (i + 1) // 2
        return jnp.where(i % 2 == 0, d, Z - d)

    @pl.loop(0, Z - 1)
    def _(i):
        to = (z + far_first(i)) % Z
        remote(feat.at[mine], zbuf.at[z], a1_send, a1_recv.at[z], k * Z + to, t)

    table[2 * blocks] = jnp.zeros((SIDE, SIDE), BF16)
    dgacc[...] = jnp.zeros_like(dgacc)
    lane = lax.broadcasted_iota(jnp.int32, (SIDE, SIDE), 1)
    lane_block = lane // (SIDE // blocks)
    count = tcount[0, 0]
    tile_copy.wait()

    @pl.loop(0, slots // GROUP)
    def _(c):
        left = jnp.concatenate([a_vm[c * GROUP + g] for g in range(GROUP)], axis=1)
        right = []
        for g in range(GROUP):
            s = c * GROUP + g
            b = jnp.where(s < count, trow[s], blocks)
            right.append(jnp.where(lane_block == b, 1.0, 0.0).astype(BF16))
        dgacc[...] += jnp.dot(left, jnp.concatenate(right, axis=0), preferred_element_type=F32)

    for b in range(blocks):
        col = jnp.sum(jnp.where(lane_block == b, dgacc[...], 0.0), axis=1, keepdims=True) * (blocks / SIDE)
        col = jnp.broadcast_to(col, (SIDE, SIDE))
        high = col.astype(BF16).astype(F32)
        deg[pl.ds(b * SIDE, SIDE), :] = col
        degs[pl.ds(b * SIDE, SIDE), :] = jnp.where(lane < SIDE // 2, high, col - high).astype(BF16)

    @pl.loop(1, T)
    def _(o):
        u = (t + o) % T
        part = pl.ds(pl.multiple_of(u * PR, PR), PR)
        remote(degs.at[part], degr.at[o - 1], g_send, g_recv, r, u)

    spot = (k * T + t) * PR
    place = (spot // SIDE, pl.ds(pl.multiple_of(spot % SIDE, PR), PR))

    def forward(source):
        wait_bytes(zbuf.at[source], a1_recv.at[source])
        remote(zbuf.at[source], table.at[place], a2_send, a2_recv, (1 - k) * Z + z, source)

        @pl.when(source != t)
        def _():
            remote(zbuf.at[source], table.at[place], a2_send, a2_recv, k * Z + z, source)

    forward(z)

    @pl.loop(0, Z - 1)
    def _(i):
        forward((z - far_first(i) + Z) % Z)

    table[place] = zbuf[t]
    wait_bytes(agg.at[pl.ds(0, (2 * T - 1) * PR // 2)], a2_recv)

    pair = 2 * SIDE
    owner_bits = (blocks * T).bit_length() - 1
    for half in range(blocks // 2):
        for j in range(2):
            agg[pl.ds((2 * half + j) * SIDE, SIDE), :] = jnp.zeros((SIDE, SIDE), F32)

        @pl.loop(0, slots // GROUP)
        def _(c):
            left = jnp.concatenate([a_vm[c * GROUP + g] for g in range(GROUP)], axis=1)
            right = []
            for g in range(GROUP):
                s = c * GROUP + g
                col = tcol[s]
                at = (col >> owner_bits) * blocks + (col & (blocks - 1))
                b = jnp.where(s < count, trow[s], blocks)
                ends = []
                for j in range(2):
                    index = jnp.where(b == 2 * half + j, at, 2 * blocks)
                    ends.append(table[index])
                right.append(jnp.concatenate(ends, axis=1))
            got = jnp.dot(left, jnp.concatenate(right, axis=0), preferred_element_type=F32)
            for j in range(2):
                agg[pl.ds((2 * half + j) * SIDE, SIDE), :] += got[:, j * SIDE:(j + 1) * SIDE]

        span = pl.ds(half * pair, pair)
        aggs[span, :] = agg[span, :].astype(BF16)
        owners = pair // PR

        @pl.loop(half * owners, (half + 1) * owners)
        def _(u):
            @pl.when(u != t)
            def _():
                part = pl.ds(pl.multiple_of(u * PR, PR), PR)
                remote(aggs.at[part], aggr.at[(u - t + T) % T - 1], p_send, p_recv, r, u)

    wait_bytes(degr, g_recv)
    degree = jnp.sum(degr[0].astype(F32), axis=1, keepdims=True)
    for o in range(1, T - 1):
        degree += jnp.sum(degr[o].astype(F32), axis=1, keepdims=True)
    degree = degree * (2.0 / SIDE) + deg[mine, :] + 1.0
    root = jnp.sqrt(degree)
    wait_bytes(aggr, p_recv)
    total = agg[mine, :]
    for o in range(T - 1):
        total += aggr[o].astype(F32)
    nbuf[mine, :] = (total / root).astype(BF16)

    @pl.loop(1, T)
    def _(o):
        remote(nbuf.at[mine], nbuf.at[mine], n_send, n_recv, r, (t + o) % T)

    w_copy.wait()
    b_copy.wait()
    c_copy.wait()
    wait_bytes(nbuf.at[pl.ds(0, (T - 1) * PR)], n_recv)

    db = None
    for b in range(blocks):
        span = pl.ds(b * SIDE, SIDE)
        pre = jnp.dot(nbuf[span, :], w_vm[...], preferred_element_type=F32) + b_vm[...]
        gate = 1.0 / (1.0 + jnp.exp(-pre))
        act_vm[span, :] = (pre * gate).astype(BF16)
        d = (c_vm[span, :].astype(F32) * gate * (1.0 + pre * (1.0 - gate))).astype(BF16)
        delta[span, :] = d
        part = jnp.sum(d.astype(F32), axis=0, keepdims=True)
        db = part if db is None else db + part
    act_copy = pltpu.make_async_copy(act_vm, act_out, act_sem)
    act_copy.start()
    dwp[...] = lax.dot_general(nbuf[...], delta[...], (((0,), (0,)), ((), ())), preferred_element_type=F32)

    SR = SIDE // T
    n = 2 * SR // Z
    own = dwp[pl.ds(pl.multiple_of(t * SR, SR), SR), :]
    for q in range(Z):
        for h in range(n):
            j = q * n + h
            piece[q, :, h * SIDE:(h + 1) * SIDE] = own[j // 2:j // 2 + 1, (j % 2) * SIDE:(j % 2 + 1) * SIDE]
        piece[q, :, n * SIDE:] = db[:, (q % 2) * SIDE:(q % 2 + 1) * SIDE]

    @pl.loop(1, R)
    def _(o):
        to = (r + o) % R
        remote(piece.at[to % Z], pieces_in.at[o - 1], d1_send, d1_recv, to, t)

    wait_bytes(pieces_in, d1_recv)
    full[z] = piece[z] + jnp.sum(pieces_in[...], axis=0)

    @pl.loop(1, Z)
    def _(o):
        remote(full.at[z], full.at[z], d2_send, d2_recv, k * Z + (z + o) % Z, t)

    wait_bytes(full.at[pl.ds(0, Z - 1)], d2_recv)
    slice_rows = pl.ds(pl.multiple_of(t * SR, SR), SR)
    lines = []
    for i in range(SR):
        halves = [full[j // n, :, (j % n) * SIDE:(j % n + 1) * SIDE] for j in (2 * i, 2 * i + 1)]
        lines.append(jnp.concatenate(halves, axis=1))
    dw_all[slice_rows, :] = jnp.concatenate(lines, axis=0)

    @pl.loop(1, T)
    def _(o):
        remote(dw_all.at[slice_rows], dw_all.at[slice_rows], e_send, e_recv, r, (t + o) % T)

    for h in range(2):
        db_out[:, h * SIDE:(h + 1) * SIDE] = full[h, :, n * SIDE:]

    wait_bytes(zbuf.at[pl.ds(0, Z - 1)], a1_send)
    wait_bytes(agg.at[pl.ds(0, (2 * T - 1) * PR // 2)], a2_send)
    wait_bytes(degr, g_send)
    wait_bytes(aggr, p_send)
    wait_bytes(nbuf.at[pl.ds(0, (T - 1) * PR)], n_send)
    wait_bytes(pieces_in, d1_send)
    wait_bytes(full.at[pl.ds(0, Z - 1)], d2_send)
    act_copy.wait()
    rest = dw_all.at[pl.ds(0, (T - 1) * SR)]
    wait_bytes(rest, e_send)
    wait_bytes(rest, e_recv)
    dw_out[...] = dw_all[...]


def per_device(T, Z, features, tile_vals, tile_row, tile_col, tile_count, weight, bias, cotangent):
    rows, width = features.shape
    slots = tile_vals.shape[2]
    hidden = weight.shape[1]
    PR = rows // T
    SR = SIDE // T
    n = 2 * SR // Z
    wide = (n + 1) * SIDE
    any_spec = pl.BlockSpec(memory_space=pl.ANY)
    hbm = pl.BlockSpec(memory_space=pltpu.HBM)
    smem = pl.BlockSpec(memory_space=pltpu.SMEM)
    vmem = pl.BlockSpec(memory_space=pltpu.VMEM)
    dma = pltpu.SemaphoreType.DMA
    V = pltpu.VMEM
    activated, dw, db = pl.pallas_call(
        functools.partial(kernel, T, Z),
        out_shape=(
            jax.ShapeDtypeStruct((rows, hidden), BF16),
            jax.ShapeDtypeStruct((width, hidden), F32),
            jax.ShapeDtypeStruct((1, hidden), F32),
        ),
        in_specs=[hbm, hbm, smem, smem, smem, hbm, hbm, hbm],
        out_specs=(any_spec, vmem, vmem),
        scratch_shapes=[
            V((slots, SIDE, SIDE), BF16),
            V((Z, PR, width), BF16),
            V((2 * rows // SIDE + 1, SIDE, width), BF16),
            V((rows, width), F32),
            V((rows, width), BF16),
            V((rows, SIDE), F32),
            V((rows, SIDE), BF16),
            V((SIDE, SIDE), F32),
            V((T - 1, PR, SIDE), BF16),
            V((T - 1, PR, width), BF16),
            V((rows, width), BF16),
            V((width, hidden), BF16),
            V((1, hidden), F32),
            V((rows, hidden), BF16),
            V((rows, hidden), BF16),
            V((rows, hidden), BF16),
            V((width, hidden), F32),
            V((Z, 1, wide), F32),
            V((2 * Z - 1, 1, wide), F32),
            V((Z, 1, wide), F32),
            V((width, hidden), F32),
            dma, dma, dma, dma,
            dma, dma((Z,)),
            dma, dma, dma, dma, dma, dma, dma, dma, dma, dma, dma, dma, dma, dma, dma,
        ],
        compiler_params=pltpu.CompilerParams(
            collective_id=0, has_side_effects=True, vmem_limit_bytes=56 * 1024 * 1024
        ),
        cost_estimate=pl.CostEstimate(
            flops=2 * slots * SIDE * SIDE * width, bytes_accessed=2 * slots * SIDE * SIDE, transcendentals=rows * hidden
        ),
    )(
        features,
        tile_vals.reshape(slots, SIDE, SIDE),
        tile_row.reshape(slots),
        tile_col.reshape(slots),
        tile_count,
        weight,
        bias.reshape(1, hidden),
        cotangent,
    )
    return activated, dw, db.reshape(hidden)


def solution(mesh):
    in_specs = (
        P("row", None),
        P("row", "team", None, None, None),
        P("row", "team", None),
        P("row", "team", None),
        P("row", "team"),
        P(),
        P(),
        P("row", None),
    )
    out_specs = (P("row", None), P(), P())
    T = mesh.shape["team"]
    Z = mesh.shape["row"] // 2
    return jax.shard_map(
        functools.partial(per_device, T, Z), mesh=mesh, in_specs=in_specs, out_specs=out_specs, check_vma=False
    )
```

```python
import functools

import jax
import jax.numpy as jnp
from jax import lax
from jax.experimental import pallas as pl
from jax.experimental.pallas import tpu as pltpu
from jax.sharding import PartitionSpec as P

MESH = pl.DeviceIdType.MESH
BF16, F32 = jnp.bfloat16, jnp.float32
SIDE = 128


def wait_bytes(ref, sem):
    pltpu.make_async_copy(ref, ref, sem).wait()


def each(count, body, first=0):
    unroll = 5

    @pl.loop(0, count // unroll)
    def _(i):
        for j in range(unroll):
            body(first + i * unroll + j)

    for j in range(count - count % unroll, count):
        body(first + j)


def kernel(
    T, Z, feat, tiles, trow, tcol, tcount, weight, bias, cot,
    act_out, dw_out, db_out,
    a_vm, up, dn, table, high, low, running, order_v, order, row_v, col_v, count_s,
    agg, aggs, deg, degs, degr, aggr, nbuf, w_vm, b_vm, c_vm,
    piece, piece_in, lined, final,
    tile_sem, row_sem, col_sem, count_sem, order_sem, w_sem, b_sem, c_sem,
    up_send, up_recv, dn_send, dn_recv, a2_send, a2_recv, g_send, g_recv, p_send, p_recv,
    n_send, n_recv, x_send, x_recv, d_send, d_recv, e_send, e_recv,
):
    R = 2 * Z
    slots = a_vm.shape[0]
    rows = nbuf.shape[0]
    blocks = rows // SIDE
    wide = 2 * blocks
    PR = rows // T
    rem = lax.rem
    r, t = lax.axis_index("row"), lax.axis_index("team")
    k, z = lax.div(r, Z), rem(r, Z)

    def remote(src, dst, ssem, rsem, row, team):
        pltpu.make_async_remote_copy(
            src_ref=src, dst_ref=dst, send_sem=ssem, recv_sem=rsem,
            device_id={"row": row, "team": team}, device_id_type=MESH,
        ).start()

    barrier = pltpu.get_barrier_semaphore()
    S = Z // 4
    near = [*range(1, S + 1), *range(Z - S, Z)]

    def signal(row, team):
        pl.semaphore_signal(barrier, inc=1, device_id={"row": row, "team": team}, device_id_type=MESH)

    def in_plane(body):
        def both(o):
            u = rem(t + o, T)
            body(0, u)
            body(1, u)

        body(1 - k, t)
        each(T - 1, both, 1)

    for o in near:
        signal(k * Z + rem(z + o, Z), t)
    in_plane(lambda kk, u: signal(kk * Z + z, u))

    row_copy = pltpu.make_async_copy(trow, row_v, row_sem)
    col_copy = pltpu.make_async_copy(tcol, col_v, col_sem)
    count_copy = pltpu.make_async_copy(tcount, count_s, count_sem)
    row_copy.start()
    col_copy.start()
    count_copy.start()
    mine = pl.ds(pl.multiple_of(t * PR, PR), PR)
    tile_copy = pltpu.make_async_copy(tiles, a_vm, tile_sem)
    tile_copy.start()
    w_copy = pltpu.make_async_copy(weight, w_vm, w_sem)
    b_copy = pltpu.make_async_copy(bias, b_vm, b_sem)
    c_copy = pltpu.make_async_copy(cot, c_vm, c_sem)
    w_copy.start()
    b_copy.start()
    c_copy.start()

    pl.semaphore_wait(barrier, len(near) + 2 * T - 1)

    ways = ((up, up_send, up_recv, 1, Z // 2), (dn, dn_send, dn_recv, -1, Z // 2 - 1))
    own_piece = feat.at[mine]
    for d in range(S, 0, -1):
        for buf, ssem, rsem, sign, far in ways:
            remote(own_piece, buf.at[d], ssem, rsem.at[d], k * Z + rem(z + sign * d + Z, Z), t)

    place = pl.ds(pl.multiple_of((k * T + t) * PR, PR), PR)

    def forward(piece_ref, source):
        remote(piece_ref, table.at[place], a2_send, a2_recv, (1 - k) * Z + z, source)

        @pl.when(source != t)
        def _():
            remote(piece_ref, table.at[place], a2_send, a2_recv, k * Z + z, source)

        @pl.when(source == t)
        def _():
            pltpu.make_async_copy(piece_ref, table.at[place], a2_recv).start()

    def relay():
        for buf, ssem, rsem, sign, far in ways:
            wait_bytes(buf.at[S], rsem.at[S])
            for e in range(far - S, 0, -1):
                remote(buf.at[S], buf.at[S + e], ssem, rsem.at[S + e], k * Z + rem(z + sign * e + Z, Z), t)

    def pass_on(distances):
        for d in distances:
            for buf, ssem, rsem, sign, far in ways:
                if d <= far:
                    if d != S:
                        wait_bytes(buf.at[d], rsem.at[d])
                    forward(buf.at[d], rem(z - sign * d + Z, Z))

    forward(own_piece, z)

    row_copy.wait()
    col_copy.wait()
    count_copy.wait()
    lane = lax.broadcasted_iota(jnp.int32, (slots, SIDE), 1)
    line = lax.broadcasted_iota(jnp.int32, (slots, SIDE), 0)
    owner_bits = (blocks * T).bit_length() - 1
    col = col_v[...]
    key = row_v[...] * wide + (col >> owner_bits) * blocks + (col & (blocks - 1))
    ids = lax.broadcasted_iota(jnp.int32, (1, slots), 1)
    key = jnp.where(ids < count_s[0, 0], key, SIDE - 1)
    key = jnp.broadcast_to(key, (slots, slots))
    slot = lax.broadcasted_iota(jnp.int32, (slots, slots), 1)
    here = lax.broadcasted_iota(jnp.int32, (slots, slots), 0)
    down = jnp.sum(jnp.where(slot == here, key, 0), axis=1, keepdims=True)
    ahead = (key < down) | ((key == down) & (slot < here))
    rank = jnp.sum(jnp.where(ahead, 1, 0), axis=1, keepdims=True)

    def across(mask, what):
        return jnp.sum(jnp.where(mask, what, 0), axis=0, keepdims=True)

    order_v[0:1, :] = across(rank == lane, line)
    key_at = across(rank == lane, down)
    key_before = across(rank + 1 == lane, down)
    order_v[1:2, :] = jnp.where((key_at == key_before) & (lane[0:1] > 0), 1, 0)
    population = across(down == lane, 1)
    order_v[2:3, :] = jnp.where(population > 0, across(down <= lane, 1) - 1, slots)
    order_copy = pltpu.make_async_copy(order_v, order, order_sem)
    order_copy.start()
    high[slots] = jnp.zeros((SIDE, SIDE), BF16)
    low[slots] = jnp.zeros((SIDE, SIDE), BF16)
    running[...] = jnp.zeros_like(running)
    relay()
    pass_on(range(S, 0, -1))
    order_copy.wait()
    tile_copy.wait()

    chunk = 8

    def sum_tiles(c):
        held = running[...]
        for g in range(chunk):
            i = c * chunk + g
            held = jnp.where(order[1, i] > 0, held, 0.0) + a_vm[order[0, i]].astype(F32)
            top = held.astype(BF16)
            high[i] = top
            low[i] = (held - top.astype(F32)).astype(BF16)
        running[...] = held

    chunks = slots // chunk
    pl.loop(0, chunks // 2)(sum_tiles)
    pass_on(range(Z // 2, S, -1))
    pl.loop(chunks // 2, chunks)(sum_tiles)

    def dense(part, half):
        bands = []
        for b in (2 * half, 2 * half + 1):
            bands.append(jnp.concatenate([part[order[2, b * wide + c]] for c in range(wide)], axis=1))
        return jnp.concatenate(bands, axis=0)

    def product(half, right):
        got = jnp.dot(dense(high, half), right, preferred_element_type=F32)
        return got + jnp.dot(dense(low, half), right, preferred_element_type=F32)

    pair = 2 * SIDE
    left_lanes = lax.broadcasted_iota(jnp.int32, (pair, SIDE), 1) < SIDE // 2
    for half in range(blocks // 2):
        span = pl.ds(half * pair, pair)
        sums = product(half, jnp.ones((wide * SIDE, SIDE), BF16))
        top = sums.astype(BF16).astype(F32)
        deg[span, :] = sums
        degs[span, :] = jnp.where(left_lanes, top, sums - top).astype(BF16)

    def give_degree(o):
        u = rem(t + o, T)
        part = pl.ds(pl.multiple_of(u * PR, PR), PR)
        remote(degs.at[part], degr.at[o - 1], g_send, g_recv, r, u)

    each(T - 1, give_degree, 1)
    wait_bytes(table, a2_recv)

    owners = pair // PR
    for half in range(blocks // 2):
        span = pl.ds(half * pair, pair)
        got = product(half, table[...])
        agg[span, :] = got
        aggs[span, :] = got.astype(BF16)

        def give_part(u):
            @pl.when(u != t)
            def _():
                part = pl.ds(pl.multiple_of(u * PR, PR), PR)
                remote(aggs.at[part], aggr.at[rem(u - t + T, T) - 1], p_send, p_recv, r, u)

        each(owners, give_part, half * owners)

    wait_bytes(degr, g_recv)
    degree = degr[0].astype(F32)
    for o in range(1, T - 1):
        degree += degr[o].astype(F32)
    degree = jnp.sum(degree, axis=1, keepdims=True) * (2.0 / SIDE) + deg[mine, :] + 1.0
    root = jnp.sqrt(degree)
    wait_bytes(aggr, p_recv)
    total = agg[mine, :]
    for o in range(T - 1):
        total += aggr[o].astype(F32)
    w_copy.wait()
    b_copy.wait()
    c_copy.wait()

    def layer(normed):
        pre = jnp.dot(normed, w_vm[...], preferred_element_type=F32) + b_vm[...]
        return pre, 1.0 / (1.0 + jnp.exp(-pre))

    normed = (total / root).astype(BF16)
    nbuf[mine, :] = normed
    pre, gate = layer(normed)
    delta = (c_vm[mine, :].astype(F32) * gate * (1.0 + pre * (1.0 - gate))).astype(BF16)
    db = jnp.sum(delta.astype(F32), axis=0, keepdims=True)
    dw = lax.dot_general(normed, delta, (((0,), (0,)), ((), ())), preferred_element_type=F32)

    SR = SIDE // T
    HR = SR // 2
    n = 2 * HR
    for q in range(2):
        for u in range(T):
            for j in range(n):
                i = u * SR + q * HR + j // 2
                piece[q * T + u, :, j * SIDE:(j + 1) * SIDE] = dw[i:i + 1, (j % 2) * SIDE:(j % 2 + 1) * SIDE]
            piece[q * T + u, :, n * SIDE:] = db[:, q * SIDE:(q + 1) * SIDE]
    mine_at = k * T + t
    in_plane(lambda kk, u: remote(piece.at[kk * T + u], piece_in.at[mine_at], x_send, x_recv, kk * Z + z, u))
    piece_in[mine_at] = piece[mine_at]
    each(T - 1, lambda o: remote(nbuf.at[mine], nbuf.at[mine], n_send, n_recv, r, rem(t + o, T)), 1)
    rest = piece_in.at[pl.ds(0, 2 * T - 1)]
    wait_bytes(rest, x_recv)
    lined[z] = jnp.sum(piece_in[...], axis=0)
    each(Z - 1, lambda o: remote(lined.at[z], lined.at[z], d_send, d_recv, k * Z + rem(z + o, Z), t), 1)

    wait_bytes(nbuf.at[pl.ds(0, (T - 1) * PR)], n_recv)
    for b in range(blocks):
        span = pl.ds(b * SIDE, SIDE)
        pre, gate = layer(nbuf[span, :])
        act_out[span, :] = (pre * gate).astype(BF16)
    wait_bytes(lined.at[pl.ds(0, Z - 1)], d_recv)
    final[mine_at] = jnp.sum(lined[...], axis=0)
    in_plane(lambda kk, u: remote(final.at[mine_at], final.at[mine_at], e_send, e_recv, kk * Z + z, u))

    wait_bytes(up.at[pl.ds(1, Z // 2)], up_send)
    wait_bytes(dn.at[pl.ds(1, Z // 2 - 1)], dn_send)
    wait_bytes(table.at[pl.ds(0, (2 * T - 1) * PR)], a2_send)
    wait_bytes(degr, g_send)
    wait_bytes(aggr, p_send)
    wait_bytes(nbuf.at[pl.ds(0, (T - 1) * PR)], n_send)
    wait_bytes(rest, x_send)
    wait_bytes(lined.at[pl.ds(0, Z - 1)], d_send)
    wait_bytes(rest, e_send)
    wait_bytes(rest, e_recv)
    for u in range(T):
        for q in range(2):
            for j in range(n):
                i = u * SR + q * HR + j // 2
                dw_out[i:i + 1, (j % 2) * SIDE:(j % 2 + 1) * SIDE] = final[q * T + u, :, j * SIDE:(j + 1) * SIDE]
    for q in range(2):
        db_out[:, q * SIDE:(q + 1) * SIDE] = final[q * T, :, n * SIDE:]


def hand_out(a, b, c, a_out, b_out, c_out, a_sem, b_sem, c_sem):
    copies = [pltpu.make_async_copy(*x) for x in ((a, a_out, a_sem), (b, b_out, b_sem), (c, c_out, c_sem))]
    for copy in copies:
        copy.start()
    for copy in copies:
        copy.wait()


def per_device(T, Z, features, tile_vals, tile_row, tile_col, tile_count, weight, bias, cotangent):
    rows, width = features.shape
    slots = tile_vals.shape[2]
    hidden = weight.shape[1]
    PR = rows // T
    SR = SIDE // T
    line = (SR + 1) * SIDE
    any_spec = pl.BlockSpec(memory_space=pl.ANY)
    vmem = pl.BlockSpec(memory_space=pltpu.VMEM)
    dma = pltpu.SemaphoreType.DMA
    V = pltpu.VMEM
    out_shape = (
        jax.ShapeDtypeStruct((rows, hidden), BF16),
        jax.ShapeDtypeStruct((width, hidden), F32),
        jax.ShapeDtypeStruct((1, hidden), F32),
    )
    results = pl.pallas_call(
        functools.partial(kernel, T, Z),
        out_shape=tuple(V(x.shape, x.dtype) for x in out_shape),
        in_specs=[any_spec] * 8,
        out_specs=(vmem,) * 3,
        scratch_shapes=[
            V((slots, SIDE, SIDE), BF16),
            V((Z // 2 + 1, PR, width), BF16),
            V((Z // 2, PR, width), BF16),
            V((2 * rows, width), BF16),
            V((slots + 1, SIDE, SIDE), BF16),
            V((slots + 1, SIDE, SIDE), BF16),
            V((SIDE, SIDE), F32),
            V((8, SIDE), jnp.int32),
            pltpu.SMEM((8, SIDE), jnp.int32),
            V((1, slots), jnp.int32),
            V((1, slots), jnp.int32),
            pltpu.SMEM((1, 1), jnp.int32),
            V((rows, width), F32),
            V((rows, width), BF16),
            V((rows, SIDE), F32),
            V((rows, SIDE), BF16),
            V((T - 1, PR, SIDE), BF16),
            V((T - 1, PR, width), BF16),
            V((rows, width), BF16),
            V((width, hidden), BF16),
            V((1, hidden), F32),
            V((rows, hidden), BF16),
            V((2 * T, 1, line), F32),
            V((2 * T, 1, line), F32),
            V((Z, 1, line), F32),
            V((2 * T, 1, line), F32),
        ]
        + [dma] * 8
        + [dma, dma((Z // 2 + 1,)), dma, dma((Z // 2 + 1,))]
        + [dma] * 14,
        compiler_params=pltpu.CompilerParams(
            collective_id=0, has_side_effects=True, vmem_limit_bytes=56 * 1024 * 1024
        ),
        cost_estimate=pl.CostEstimate(
            flops=2 * slots * SIDE * SIDE * width, bytes_accessed=2 * slots * SIDE * SIDE, transcendentals=rows * hidden
        ),
    )(
        features,
        tile_vals.reshape(slots, SIDE, SIDE),
        tile_row.reshape(1, slots),
        tile_col.reshape(1, slots),
        tile_count,
        weight,
        bias.reshape(1, hidden),
        cotangent,
    )
    activated, dw, db = pl.pallas_call(
        hand_out,
        out_shape=out_shape,
        in_specs=[vmem] * 3,
        out_specs=(any_spec,) * 3,
        scratch_shapes=[dma] * 3,
        compiler_params=pltpu.CompilerParams(vmem_limit_bytes=56 * 1024 * 1024),
    )(*(pltpu.with_memory_space_constraint(x, pltpu.VMEM) for x in results))
    return activated, dw, db.reshape(hidden)


def solution(mesh):
    in_specs = (
        P("row", None),
        P("row", "team", None, None, None),
        P("row", "team", None),
        P("row", "team", None),
        P("row", "team"),
        P(),
        P(),
        P("row", None),
    )
    out_specs = (P("row", None), P(), P())
    T = mesh.shape["team"]
    Z = mesh.shape["row"] // 2
    return jax.shard_map(
        functools.partial(per_device, T, Z), mesh=mesh, in_specs=in_specs, out_specs=out_specs, check_vma=False
    )
```

```python
import functools

import jax
import jax.numpy as jnp
from jax import lax
from jax.experimental import pallas as pl
from jax.experimental.pallas import tpu as pltpu
from jax.sharding import PartitionSpec as P

MESH = pl.DeviceIdType.MESH
BF16, F32 = jnp.bfloat16, jnp.float32
SIDE = 128


def wait_bytes(ref, sem):
    pltpu.make_async_copy(ref, ref, sem).wait()


def each(count, body, first=0):
    unroll = 5

    @pl.loop(0, count // unroll)
    def _(i):
        for j in range(unroll):
            body(first + i * unroll + j)

    for j in range(count - count % unroll, count):
        body(first + j)


def kernel(
    T, Z, feat, tiles, trow, tcol, tcount, weight, bias, cot,
    act_out, dw_out, db_out,
    a_vm, up, dn, table, high, low, running, order_v, order, row_v, col_v, count_s,
    agg, aggs, degs, degr, aggr, nbuf, w_vm, b_vm, c_vm,
    piece, piece_in, lined, final,
    tile_sem, row_sem, col_sem, count_sem, order_sem, w_sem, b_sem, c_sem,
    up_send, up_recv, dn_send, dn_recv, a2_send, a2_recv, g_send, g_recv, p_send, p_recv,
    n_send, n_recv, x_send, x_recv, d_send, d_recv, e_send, e_recv,
):
    R = 2 * Z
    slots = a_vm.shape[0]
    rows = nbuf.shape[0]
    blocks = rows // SIDE
    wide = 2 * blocks
    PR = rows // T
    rem = lax.rem
    r, t = lax.axis_index("row"), lax.axis_index("team")
    k, z = lax.div(r, Z), rem(r, Z)

    def remote(src, dst, ssem, rsem, row, team):
        pltpu.make_async_remote_copy(
            src_ref=src, dst_ref=dst, send_sem=ssem, recv_sem=rsem,
            device_id={"row": row, "team": team}, device_id_type=MESH,
        ).start()

    barrier = pltpu.get_barrier_semaphore()
    S = Z // 4
    near = [*range(1, S + 1), *range(Z - S, Z)]

    def signal(row, team):
        pl.semaphore_signal(barrier, inc=1, device_id={"row": row, "team": team}, device_id_type=MESH)

    def in_plane(body):
        def both(o):
            u = rem(t + o, T)
            body(0, u)
            body(1, u)

        body(1 - k, t)
        each(T - 1, both, 1)

    for o in near:
        signal(k * Z + rem(z + o, Z), t)
    in_plane(lambda kk, u: signal(kk * Z + z, u))

    row_copy = pltpu.make_async_copy(trow, row_v, row_sem)
    col_copy = pltpu.make_async_copy(tcol, col_v, col_sem)
    count_copy = pltpu.make_async_copy(tcount, count_s, count_sem)
    row_copy.start()
    col_copy.start()
    count_copy.start()
    mine = pl.ds(pl.multiple_of(t * PR, PR), PR)
    tile_copy = pltpu.make_async_copy(tiles, a_vm, tile_sem)
    w_copy = pltpu.make_async_copy(weight, w_vm, w_sem)
    b_copy = pltpu.make_async_copy(bias, b_vm, b_sem)
    c_copy = pltpu.make_async_copy(cot, c_vm, c_sem)

    pl.semaphore_wait(barrier, len(near) + 2 * T - 1)

    ways = ((up, up_send, up_recv, 1, Z // 2), (dn, dn_send, dn_recv, -1, Z // 2 - 1))
    own_piece = feat.at[mine]
    for d in range(S, 0, -1):
        for buf, ssem, rsem, sign, far in ways:
            remote(own_piece, buf.at[d], ssem, rsem.at[d], k * Z + rem(z + sign * d + Z, Z), t)

    place = pl.ds(pl.multiple_of((k * T + t) * PR, PR), PR)

    def forward(piece_ref, source):
        remote(piece_ref, table.at[place], a2_send, a2_recv, (1 - k) * Z + z, source)

        @pl.when(source != t)
        def _():
            remote(piece_ref, table.at[place], a2_send, a2_recv, k * Z + z, source)

        @pl.when(source == t)
        def _():
            pltpu.make_async_copy(piece_ref, table.at[place], a2_recv).start()

    def relay():
        for buf, ssem, rsem, sign, far in ways:
            wait_bytes(buf.at[S], rsem.at[S])
            for e in range(far - S, 0, -1):
                remote(buf.at[S], buf.at[S + e], ssem, rsem.at[S + e], k * Z + rem(z + sign * e + Z, Z), t)

    def pass_on(distances):
        for d in distances:
            for buf, ssem, rsem, sign, far in ways:
                if d <= far:
                    if d != S:
                        wait_bytes(buf.at[d], rsem.at[d])
                    forward(buf.at[d], rem(z - sign * d + Z, Z))

    forward(own_piece, z)
    tile_copy.start()

    row_copy.wait()
    col_copy.wait()
    count_copy.wait()
    lane = lax.broadcasted_iota(jnp.int32, (slots, SIDE), 1)
    line = lax.broadcasted_iota(jnp.int32, (slots, SIDE), 0)
    owner_bits = (blocks * T).bit_length() - 1
    col = col_v[...]
    key = row_v[...] * wide + (col >> owner_bits) * blocks + (col & (blocks - 1))
    ids = lax.broadcasted_iota(jnp.int32, (1, slots), 1)
    key = jnp.where(ids < count_s[0, 0], key, SIDE - 1)
    key = jnp.broadcast_to(key, (slots, slots))
    slot = lax.broadcasted_iota(jnp.int32, (slots, slots), 1)
    here = lax.broadcasted_iota(jnp.int32, (slots, slots), 0)
    down = jnp.sum(jnp.where(slot == here, key, 0), axis=1, keepdims=True)
    ahead = (key < down) | ((key == down) & (slot < here))
    rank = jnp.sum(jnp.where(ahead, 1, 0), axis=1, keepdims=True)

    def across(mask, what):
        return jnp.sum(jnp.where(mask, what, 0), axis=0, keepdims=True)

    order_v[0:1, :] = across(rank == lane, line)
    key_at = across(rank == lane, down)
    key_before = across(rank + 1 == lane, down)
    order_v[1:2, :] = jnp.where((key_at == key_before) & (lane[0:1] > 0), 1, 0)
    population = across(down == lane, 1)
    order_v[2:3, :] = jnp.where(population > 0, across(down <= lane, 1) - 1, slots)
    order_copy = pltpu.make_async_copy(order_v, order, order_sem)
    order_copy.start()
    high[slots] = jnp.zeros((SIDE, SIDE), BF16)
    low[slots] = jnp.zeros((SIDE, SIDE), BF16)
    running[...] = jnp.zeros_like(running)
    relay()
    w_copy.start()
    b_copy.start()
    c_copy.start()
    pass_on(range(S, 0, -1))
    order_copy.wait()
    tile_copy.wait()

    chunk = 8

    def sum_tiles(c):
        held = running[...]
        for g in range(chunk):
            i = c * chunk + g
            held = jnp.where(order[1, i] > 0, held, 0.0) + a_vm[order[0, i]].astype(F32)
            top = held.astype(BF16)
            high[i] = top
            low[i] = (held - top.astype(F32)).astype(BF16)
        running[...] = held

    chunks = slots // chunk
    pl.loop(0, chunks // 2)(sum_tiles)
    pass_on(range(Z // 2, S, -1))
    pl.loop(chunks // 2, chunks)(sum_tiles)

    def dense(part, half):
        bands = []
        for b in (2 * half, 2 * half + 1):
            bands.append(jnp.concatenate([part[order[2, b * wide + c]] for c in range(wide)], axis=1))
        return jnp.concatenate(bands, axis=0)

    def product(half, right):
        got = jnp.dot(dense(high, half), right, preferred_element_type=F32)
        return got + jnp.dot(dense(low, half), right, preferred_element_type=F32)

    pair = 2 * SIDE
    across_lane = lax.broadcasted_iota(jnp.int32, (SIDE, SIDE), 1)
    down_line = lax.broadcasted_iota(jnp.int32, (SIDE, SIDE), 0)
    for half in range(blocks // 2):
        sums = product(half, jnp.ones((wide * SIDE, SIDE), BF16))
        for j in range(2):
            square = jnp.where(across_lane == down_line, sums[j * SIDE:(j + 1) * SIDE, :], 0.0)
            degs[2 * half + j] = jnp.sum(square, axis=0, keepdims=True)

    def give_degree(o):
        u = rem(t + o, T)
        remote(degs.at[lax.div(u * PR, SIDE)], degr.at[o - 1], g_send, g_recv, r, u)

    each(T - 1, give_degree, 1)
    wait_bytes(table, a2_recv)

    owners = pair // PR
    for half in range(blocks // 2):
        span = pl.ds(half * pair, pair)
        got = product(half, table[...])
        agg[span, :] = got
        aggs[span, :] = got.astype(BF16)

        def give_part(u):
            @pl.when(u != t)
            def _():
                part = pl.ds(pl.multiple_of(u * PR, PR), PR)
                remote(aggs.at[part], aggr.at[rem(u - t + T, T) - 1], p_send, p_recv, r, u)

        each(owners, give_part, half * owners)

    wait_bytes(degr, g_recv)
    degree = degs[lax.div(t * PR, SIDE)] + jnp.sum(degr[...], axis=0) + 1.0
    here = lax.broadcasted_iota(jnp.int32, (PR, SIDE), 0) + rem(t * PR, SIDE)
    here = here == lax.broadcasted_iota(jnp.int32, (PR, SIDE), 1)
    degree = jnp.sum(jnp.where(here, degree, 0.0), axis=1, keepdims=True)
    root = jnp.sqrt(degree)
    wait_bytes(aggr, p_recv)
    total = agg[mine, :]
    for o in range(T - 1):
        total += aggr[o].astype(F32)
    w_copy.wait()
    b_copy.wait()
    c_copy.wait()

    def layer(normed):
        pre = jnp.dot(normed, w_vm[...], preferred_element_type=F32) + b_vm[...]
        return pre, 1.0 / (1.0 + jnp.exp(-pre))

    normed = (total / root).astype(BF16)
    nbuf[mine, :] = normed
    pre, gate = layer(normed)
    delta = (c_vm[mine, :].astype(F32) * gate * (1.0 + pre * (1.0 - gate))).astype(BF16)
    db = jnp.sum(delta.astype(F32), axis=0, keepdims=True)
    dw = lax.dot_general(normed, delta, (((0,), (0,)), ((), ())), preferred_element_type=F32)

    SR = SIDE // T
    HR = SR // 2
    n = 2 * HR
    for q in range(2):
        for u in range(T):
            for j in range(n):
                i = u * SR + q * HR + j // 2
                piece[q * T + u, :, j * SIDE:(j + 1) * SIDE] = dw[i:i + 1, (j % 2) * SIDE:(j % 2 + 1) * SIDE]
            piece[q * T + u, :, n * SIDE:] = db[:, q * SIDE:(q + 1) * SIDE]
    mine_at = k * T + t
    in_plane(lambda kk, u: remote(piece.at[kk * T + u], piece_in.at[mine_at], x_send, x_recv, kk * Z + z, u))
    piece_in[mine_at] = piece[mine_at]
    rest = piece_in.at[pl.ds(0, 2 * T - 1)]
    wait_bytes(rest, x_recv)
    lined[z] = jnp.sum(piece_in[...], axis=0)
    each(Z - 1, lambda o: remote(lined.at[z], lined.at[z], d_send, d_recv, k * Z + rem(z + o, Z), t), 1)
    each(T - 1, lambda o: remote(nbuf.at[mine], nbuf.at[mine], n_send, n_recv, r, rem(t + o, T)), 1)
    wait_bytes(lined.at[pl.ds(0, Z - 1)], d_recv)
    final[mine_at] = jnp.sum(lined[...], axis=0)
    in_plane(lambda kk, u: remote(final.at[mine_at], final.at[mine_at], e_send, e_recv, kk * Z + z, u))

    wait_bytes(nbuf.at[pl.ds(0, (T - 1) * PR)], n_recv)
    for b in range(blocks):
        span = pl.ds(b * SIDE, SIDE)
        pre, gate = layer(nbuf[span, :])
        act_out[span, :] = (pre * gate).astype(BF16)

    wait_bytes(up.at[pl.ds(1, Z // 2)], up_send)
    wait_bytes(dn.at[pl.ds(1, Z // 2 - 1)], dn_send)
    wait_bytes(table.at[pl.ds(0, (2 * T - 1) * PR)], a2_send)
    wait_bytes(degr, g_send)
    wait_bytes(aggr, p_send)
    wait_bytes(nbuf.at[pl.ds(0, (T - 1) * PR)], n_send)
    wait_bytes(rest, x_send)
    wait_bytes(lined.at[pl.ds(0, Z - 1)], d_send)
    wait_bytes(rest, e_send)
    wait_bytes(rest, e_recv)
    for u in range(T):
        for q in range(2):
            for j in range(n):
                i = u * SR + q * HR + j // 2
                dw_out[i:i + 1, (j % 2) * SIDE:(j % 2 + 1) * SIDE] = final[q * T + u, :, j * SIDE:(j + 1) * SIDE]
    for q in range(2):
        db_out[:, q * SIDE:(q + 1) * SIDE] = final[q * T, :, n * SIDE:]


def hand_out(a, b, c, a_out, b_out, c_out, a_sem, b_sem, c_sem):
    copies = [pltpu.make_async_copy(*x) for x in ((a, a_out, a_sem), (b, b_out, b_sem), (c, c_out, c_sem))]
    for copy in copies:
        copy.start()
    for copy in copies:
        copy.wait()


def per_device(T, Z, features, tile_vals, tile_row, tile_col, tile_count, weight, bias, cotangent):
    rows, width = features.shape
    slots = tile_vals.shape[2]
    hidden = weight.shape[1]
    PR = rows // T
    SR = SIDE // T
    line = (SR + 1) * SIDE
    any_spec = pl.BlockSpec(memory_space=pl.ANY)
    vmem = pl.BlockSpec(memory_space=pltpu.VMEM)
    dma = pltpu.SemaphoreType.DMA
    V = pltpu.VMEM
    out_shape = (
        jax.ShapeDtypeStruct((rows, hidden), BF16),
        jax.ShapeDtypeStruct((width, hidden), F32),
        jax.ShapeDtypeStruct((1, hidden), F32),
    )
    results = pl.pallas_call(
        functools.partial(kernel, T, Z),
        out_shape=tuple(V(x.shape, x.dtype) for x in out_shape),
        in_specs=[any_spec] * 8,
        out_specs=(vmem,) * 3,
        scratch_shapes=[
            V((slots, SIDE, SIDE), BF16),
            V((Z // 2 + 1, PR, width), BF16),
            V((Z // 2, PR, width), BF16),
            V((2 * rows, width), BF16),
            V((slots + 1, SIDE, SIDE), BF16),
            V((slots + 1, SIDE, SIDE), BF16),
            V((SIDE, SIDE), F32),
            V((8, SIDE), jnp.int32),
            pltpu.SMEM((8, SIDE), jnp.int32),
            V((1, slots), jnp.int32),
            V((1, slots), jnp.int32),
            pltpu.SMEM((1, 1), jnp.int32),
            V((rows, width), F32),
            V((rows, width), BF16),
            V((rows // SIDE, 1, SIDE), F32),
            V((T - 1, 1, SIDE), F32),
            V((T - 1, PR, width), BF16),
            V((rows, width), BF16),
            V((width, hidden), BF16),
            V((1, hidden), F32),
            V((rows, hidden), BF16),
            V((2 * T, 1, line), F32),
            V((2 * T, 1, line), F32),
            V((Z, 1, line), F32),
            V((2 * T, 1, line), F32),
        ]
        + [dma] * 8
        + [dma, dma((Z // 2 + 1,)), dma, dma((Z // 2 + 1,))]
        + [dma] * 14,
        compiler_params=pltpu.CompilerParams(
            collective_id=0, has_side_effects=True, vmem_limit_bytes=56 * 1024 * 1024
        ),
        cost_estimate=pl.CostEstimate(
            flops=2 * slots * SIDE * SIDE * width, bytes_accessed=2 * slots * SIDE * SIDE, transcendentals=rows * hidden
        ),
    )(
        features,
        tile_vals.reshape(slots, SIDE, SIDE),
        tile_row.reshape(1, slots),
        tile_col.reshape(1, slots),
        tile_count,
        weight,
        bias.reshape(1, hidden),
        cotangent,
    )
    activated, dw, db = pl.pallas_call(
        hand_out,
        out_shape=out_shape,
        in_specs=[vmem] * 3,
        out_specs=(any_spec,) * 3,
        scratch_shapes=[dma] * 3,
        compiler_params=pltpu.CompilerParams(vmem_limit_bytes=56 * 1024 * 1024),
    )(*(pltpu.with_memory_space_constraint(x, pltpu.VMEM) for x in results))
    return activated, dw, db.reshape(hidden)


def solution(mesh):
    in_specs = (
        P("row", None),
        P("row", "team", None, None, None),
        P("row", "team", None),
        P("row", "team", None),
        P("row", "team"),
        P(),
        P(),
        P("row", None),
    )
    out_specs = (P("row", None), P(), P())
    T = mesh.shape["team"]
    Z = mesh.shape["row"] // 2
    return jax.shard_map(
        functools.partial(per_device, T, Z), mesh=mesh, in_specs=in_specs, out_specs=out_specs, check_vma=False
    )
```

```python
import functools

import jax
import jax.numpy as jnp
from jax import lax
from jax.experimental import pallas as pl
from jax.experimental.pallas import tpu as pltpu
from jax.sharding import PartitionSpec as P

MESH = pl.DeviceIdType.MESH
BF16, F32 = jnp.bfloat16, jnp.float32
SIDE = 128


def wait_bytes(ref, sem):
    pltpu.make_async_copy(ref, ref, sem).wait()


def each(count, body, first=0):
    unroll = 5

    @pl.loop(0, count // unroll)
    def _(i):
        for j in range(unroll):
            body(first + i * unroll + j)

    for j in range(count - count % unroll, count):
        body(first + j)


def kernel(
    T, Z, feat, tiles, trow, tcol, tcount, weight, bias, cot,
    act_out, dw_out, db_out,
    a_vm, up, dn, table, high, low, running, order_v, order, row_v, col_v, count_s,
    agg, aggs, aggr, nbuf, w_vm, b_vm, c_vm,
    piece, piece_in, lined, final,
    tile_sem, row_sem, col_sem, count_sem, order_sem, w_sem, b_sem, c_sem,
    up_send, up_recv, dn_send, dn_recv, a2_send, a2_recv, p_send, p_recv,
    n_send, n_recv, x_send, x_recv, d_send, d_recv, e_send, e_recv,
):
    R = 2 * Z
    slots = a_vm.shape[0]
    rows = nbuf.shape[0]
    blocks = rows // SIDE
    wide = 2 * blocks
    PR = rows // T
    rem = lax.rem
    r, t = lax.axis_index("row"), lax.axis_index("team")
    k, z = lax.div(r, Z), rem(r, Z)

    def remote(src, dst, ssem, rsem, row, team):
        pltpu.make_async_remote_copy(
            src_ref=src, dst_ref=dst, send_sem=ssem, recv_sem=rsem,
            device_id={"row": row, "team": team}, device_id_type=MESH,
        ).start()

    barrier = pltpu.get_barrier_semaphore()
    S = Z // 4
    near = [*range(1, S + 1), *range(Z - S, Z)]

    def signal(row, team):
        pl.semaphore_signal(barrier, inc=1, device_id={"row": row, "team": team}, device_id_type=MESH)

    def in_plane(body):
        def both(o):
            u = rem(t + o, T)
            body(0, u)
            body(1, u)

        body(1 - k, t)
        each(T - 1, both, 1)

    for o in near:
        signal(k * Z + rem(z + o, Z), t)
    in_plane(lambda kk, u: signal(kk * Z + z, u))

    row_copy = pltpu.make_async_copy(trow, row_v, row_sem)
    col_copy = pltpu.make_async_copy(tcol, col_v, col_sem)
    count_copy = pltpu.make_async_copy(tcount, count_s, count_sem)
    row_copy.start()
    col_copy.start()
    count_copy.start()
    mine = pl.ds(pl.multiple_of(t * PR, PR), PR)
    tile_copy = pltpu.make_async_copy(tiles, a_vm, tile_sem)
    w_copy = pltpu.make_async_copy(weight, w_vm, w_sem)
    b_copy = pltpu.make_async_copy(bias, b_vm, b_sem)
    c_copy = pltpu.make_async_copy(cot, c_vm, c_sem)

    pl.semaphore_wait(barrier, len(near) + 2 * T - 1)

    ways = ((up, up_send, up_recv, 1, Z // 2), (dn, dn_send, dn_recv, -1, Z // 2 - 1))
    own_piece = feat.at[mine]
    for d in range(S, 0, -1):
        for buf, ssem, rsem, sign, far in ways:
            remote(own_piece, buf.at[d], ssem, rsem.at[d], k * Z + rem(z + sign * d + Z, Z), t)

    place = pl.ds(pl.multiple_of((k * T + t) * PR, PR), PR)

    def forward(piece_ref, source):
        remote(piece_ref, table.at[place], a2_send, a2_recv, (1 - k) * Z + z, source)

        @pl.when(source != t)
        def _():
            remote(piece_ref, table.at[place], a2_send, a2_recv, k * Z + z, source)

        @pl.when(source == t)
        def _():
            pltpu.make_async_copy(piece_ref, table.at[place], a2_recv).start()

    def relay():
        for buf, ssem, rsem, sign, far in ways:
            wait_bytes(buf.at[S], rsem.at[S])
            for e in range(far - S, 0, -1):
                remote(buf.at[S], buf.at[S + e], ssem, rsem.at[S + e], k * Z + rem(z + sign * e + Z, Z), t)

    def pass_on(distances):
        for d in distances:
            for buf, ssem, rsem, sign, far in ways:
                if d <= far:
                    if d != S:
                        wait_bytes(buf.at[d], rsem.at[d])
                    forward(buf.at[d], rem(z - sign * d + Z, Z))

    forward(own_piece, z)
    tile_copy.start()

    row_copy.wait()
    col_copy.wait()
    count_copy.wait()
    lane = lax.broadcasted_iota(jnp.int32, (slots, SIDE), 1)
    line = lax.broadcasted_iota(jnp.int32, (slots, SIDE), 0)
    owner_bits = (blocks * T).bit_length() - 1
    col = col_v[...]
    key = row_v[...] * wide + (col >> owner_bits) * blocks + (col & (blocks - 1))
    ids = lax.broadcasted_iota(jnp.int32, (1, slots), 1)
    key = jnp.where(ids < count_s[0, 0], key, SIDE - 1)
    key = jnp.broadcast_to(key, (slots, slots))
    slot = lax.broadcasted_iota(jnp.int32, (slots, slots), 1)
    here = lax.broadcasted_iota(jnp.int32, (slots, slots), 0)
    down = jnp.sum(jnp.where(slot == here, key, 0), axis=1, keepdims=True)
    ahead = (key < down) | ((key == down) & (slot < here))
    rank = jnp.sum(jnp.where(ahead, 1, 0), axis=1, keepdims=True)

    def across(mask, what):
        return jnp.sum(jnp.where(mask, what, 0), axis=0, keepdims=True)

    order_v[0:1, :] = across(rank == lane, line)
    key_at = across(rank == lane, down)
    key_before = across(rank + 1 == lane, down)
    order_v[1:2, :] = jnp.where((key_at == key_before) & (lane[0:1] > 0), 1, 0)
    population = across(down == lane, 1)
    order_v[2:3, :] = jnp.where(population > 0, across(down <= lane, 1) - 1, slots)
    order_copy = pltpu.make_async_copy(order_v, order, order_sem)
    order_copy.start()
    high[slots] = jnp.zeros((SIDE, SIDE), BF16)
    low[slots] = jnp.zeros((SIDE, SIDE), BF16)
    running[...] = jnp.zeros_like(running)
    relay()
    w_copy.start()
    b_copy.start()
    c_copy.start()
    pass_on(range(S, 0, -1))
    order_copy.wait()
    tile_copy.wait()

    chunk = 8

    def sum_tiles(c):
        held = running[...]
        for g in range(chunk):
            i = c * chunk + g
            held = jnp.where(order[1, i] > 0, held, 0.0) + a_vm[order[0, i]].astype(F32)
            top = held.astype(BF16)
            high[i] = top
            low[i] = (held - top.astype(F32)).astype(BF16)
        running[...] = held

    chunks = slots // chunk
    early = 3 * chunks // 8
    pl.loop(0, early)(sum_tiles)
    pass_on(range(Z // 2, S, -1))
    pl.loop(early, chunks)(sum_tiles)

    def dense(part, half):
        bands = []
        for b in (2 * half, 2 * half + 1):
            bands.append(jnp.concatenate([part[order[2, b * wide + c]] for c in range(wide)], axis=1))
        return jnp.concatenate(bands, axis=0)

    def product(half, right):
        got = jnp.dot(dense(high, half), right, preferred_element_type=F32)
        return got + jnp.dot(dense(low, half), right, preferred_element_type=F32)

    wait_bytes(table, a2_recv)

    pair = 2 * SIDE
    owners = pair // PR
    PD = PR // 2
    quarter = lax.broadcasted_iota(jnp.int32, (PD, SIDE), 1) // (SIDE // 4)
    right = jnp.concatenate([table[...], jnp.ones((wide * SIDE, SIDE), BF16)], axis=1)
    for half in range(blocks // 2):
        got = product(half, right)
        agg[pl.ds(half * pair, pair), :] = got[:, :SIDE]
        for v in range(owners):
            u = half * owners + v
            aggs[u, 0:PR, :] = got[v * PR:(v + 1) * PR, :SIDE].astype(BF16)
            sums = jnp.where(quarter < 2, got[v * PR:v * PR + PD, SIDE:], got[v * PR + PD:(v + 1) * PR, SIDE:])
            top = sums.astype(BF16).astype(F32)
            aggs[u, PR:, :] = jnp.where((quarter == 0) | (quarter == 2), top, sums - top).astype(BF16)

        def give_part(u):
            @pl.when(u != t)
            def _():
                remote(aggs.at[u], aggr.at[rem(u - t + T, T) - 1], p_send, p_recv, r, u)

        each(owners, give_part, half * owners)

    wait_bytes(aggr, p_recv)
    total = agg[mine, :]
    parts = aggs[t, PR:, :].astype(F32)
    for o in range(T - 1):
        total += aggr[o, 0:PR, :].astype(F32)
        parts += aggr[o, PR:, :].astype(F32)
    ends = [jnp.sum(jnp.where(quarter // 2 == q, parts, 0.0), axis=1, keepdims=True) for q in range(2)]
    root = jnp.sqrt(jnp.concatenate(ends, axis=0) * (4.0 / SIDE) + 1.0)
    w_copy.wait()
    b_copy.wait()
    c_copy.wait()

    def layer(normed):
        pre = jnp.dot(normed, w_vm[...], preferred_element_type=F32) + b_vm[...]
        return pre, 1.0 / (1.0 + jnp.exp(-pre))

    normed = (total / root).astype(BF16)
    nbuf[mine, :] = normed
    pre, gate = layer(normed)
    delta = (c_vm[mine, :].astype(F32) * gate * (1.0 + pre * (1.0 - gate))).astype(BF16)
    db = jnp.sum(delta.astype(F32), axis=0, keepdims=True)
    dw = lax.dot_general(normed, delta, (((0,), (0,)), ((), ())), preferred_element_type=F32)

    SR = SIDE // T
    HR = SR // 2
    n = 2 * HR
    for q in range(2):
        for u in range(T):
            for j in range(n):
                i = u * SR + q * HR + j // 2
                piece[q * T + u, :, j * SIDE:(j + 1) * SIDE] = dw[i:i + 1, (j % 2) * SIDE:(j % 2 + 1) * SIDE]
            piece[q * T + u, :, n * SIDE:] = db[:, q * SIDE:(q + 1) * SIDE]
    mine_at = k * T + t
    in_plane(lambda kk, u: remote(piece.at[kk * T + u], piece_in.at[mine_at], x_send, x_recv, kk * Z + z, u))
    piece_in[mine_at] = piece[mine_at]
    rest = piece_in.at[pl.ds(0, 2 * T - 1)]
    wait_bytes(rest, x_recv)
    lined[z] = jnp.sum(piece_in[...], axis=0)
    each(Z - 1, lambda o: remote(lined.at[z], lined.at[z], d_send, d_recv, k * Z + rem(z + o, Z), t), 1)
    each(T - 1, lambda o: remote(nbuf.at[mine], nbuf.at[mine], n_send, n_recv, r, rem(t + o, T)), 1)
    wait_bytes(lined.at[pl.ds(0, Z - 1)], d_recv)
    final[mine_at] = jnp.sum(lined[...], axis=0)
    in_plane(lambda kk, u: remote(final.at[mine_at], final.at[mine_at], e_send, e_recv, kk * Z + z, u))

    wait_bytes(nbuf.at[pl.ds(0, (T - 1) * PR)], n_recv)
    for b in range(blocks):
        span = pl.ds(b * SIDE, SIDE)
        pre, gate = layer(nbuf[span, :])
        act_out[span, :] = (pre * gate).astype(BF16)

    wait_bytes(up.at[pl.ds(1, Z // 2)], up_send)
    wait_bytes(dn.at[pl.ds(1, Z // 2 - 1)], dn_send)
    wait_bytes(table.at[pl.ds(0, (2 * T - 1) * PR)], a2_send)
    wait_bytes(aggr, p_send)
    wait_bytes(nbuf.at[pl.ds(0, (T - 1) * PR)], n_send)
    wait_bytes(rest, x_send)
    wait_bytes(lined.at[pl.ds(0, Z - 1)], d_send)
    wait_bytes(rest, e_send)
    wait_bytes(rest, e_recv)
    for u in range(T):
        for q in range(2):
            for j in range(n):
                i = u * SR + q * HR + j // 2
                dw_out[i:i + 1, (j % 2) * SIDE:(j % 2 + 1) * SIDE] = final[q * T + u, :, j * SIDE:(j + 1) * SIDE]
    for q in range(2):
        db_out[:, q * SIDE:(q + 1) * SIDE] = final[q * T, :, n * SIDE:]


def hand_out(a, b, c, a_out, b_out, c_out, a_sem, b_sem, c_sem):
    copies = [pltpu.make_async_copy(*x) for x in ((a, a_out, a_sem), (b, b_out, b_sem), (c, c_out, c_sem))]
    for copy in copies:
        copy.start()
    for copy in copies:
        copy.wait()


def per_device(T, Z, features, tile_vals, tile_row, tile_col, tile_count, weight, bias, cotangent):
    rows, width = features.shape
    slots = tile_vals.shape[2]
    hidden = weight.shape[1]
    PR = rows // T
    SR = SIDE // T
    line = (SR + 1) * SIDE
    any_spec = pl.BlockSpec(memory_space=pl.ANY)
    vmem = pl.BlockSpec(memory_space=pltpu.VMEM)
    dma = pltpu.SemaphoreType.DMA
    V = pltpu.VMEM
    out_shape = (
        jax.ShapeDtypeStruct((rows, hidden), BF16),
        jax.ShapeDtypeStruct((width, hidden), F32),
        jax.ShapeDtypeStruct((1, hidden), F32),
    )
    results = pl.pallas_call(
        functools.partial(kernel, T, Z),
        out_shape=tuple(V(x.shape, x.dtype) for x in out_shape),
        in_specs=[any_spec] * 8,
        out_specs=(vmem,) * 3,
        scratch_shapes=[
            V((slots, SIDE, SIDE), BF16),
            V((Z // 2 + 1, PR, width), BF16),
            V((Z // 2, PR, width), BF16),
            V((2 * rows, width), BF16),
            V((slots + 1, SIDE, SIDE), BF16),
            V((slots + 1, SIDE, SIDE), BF16),
            V((SIDE, SIDE), F32),
            V((8, SIDE), jnp.int32),
            pltpu.SMEM((8, SIDE), jnp.int32),
            V((1, slots), jnp.int32),
            V((1, slots), jnp.int32),
            pltpu.SMEM((1, 1), jnp.int32),
            V((rows, width), F32),
            V((T, PR + PR // 2, width), BF16),
            V((T - 1, PR + PR // 2, width), BF16),
            V((rows, width), BF16),
            V((width, hidden), BF16),
            V((1, hidden), F32),
            V((rows, hidden), BF16),
            V((2 * T, 1, line), F32),
            V((2 * T, 1, line), F32),
            V((Z, 1, line), F32),
            V((2 * T, 1, line), F32),
        ]
        + [dma] * 8
        + [dma, dma((Z // 2 + 1,)), dma, dma((Z // 2 + 1,))]
        + [dma] * 12,
        compiler_params=pltpu.CompilerParams(
            collective_id=0, has_side_effects=True, vmem_limit_bytes=56 * 1024 * 1024
        ),
        cost_estimate=pl.CostEstimate(
            flops=2 * slots * SIDE * SIDE * width, bytes_accessed=2 * slots * SIDE * SIDE, transcendentals=rows * hidden
        ),
    )(
        features,
        tile_vals.reshape(slots, SIDE, SIDE),
        tile_row.reshape(1, slots),
        tile_col.reshape(1, slots),
        tile_count,
        weight,
        bias.reshape(1, hidden),
        cotangent,
    )
    activated, dw, db = pl.pallas_call(
        hand_out,
        out_shape=out_shape,
        in_specs=[vmem] * 3,
        out_specs=(any_spec,) * 3,
        scratch_shapes=[dma] * 3,
        compiler_params=pltpu.CompilerParams(vmem_limit_bytes=56 * 1024 * 1024),
    )(*(pltpu.with_memory_space_constraint(x, pltpu.VMEM) for x in results))
    return activated, dw, db.reshape(hidden)


def solution(mesh):
    in_specs = (
        P("row", None),
        P("row", "team", None, None, None),
        P("row", "team", None),
        P("row", "team", None),
        P("row", "team"),
        P(),
        P(),
        P("row", None),
    )
    out_specs = (P("row", None), P(), P())
    T = mesh.shape["team"]
    Z = mesh.shape["row"] // 2
    return jax.shard_map(
        functools.partial(per_device, T, Z), mesh=mesh, in_specs=in_specs, out_specs=out_specs, check_vma=False
    )
```

```python
import functools

import jax
import jax.numpy as jnp
from jax import lax
from jax.experimental import pallas as pl
from jax.experimental.pallas import tpu as pltpu
from jax.sharding import PartitionSpec as P

MESH = pl.DeviceIdType.MESH
BF16, F32 = jnp.bfloat16, jnp.float32
SIDE = 128


def wait_bytes(ref, sem):
    pltpu.make_async_copy(ref, ref, sem).wait()


def each(count, body, first=0):
    unroll = 5

    @pl.loop(0, count // unroll)
    def _(i):
        for j in range(unroll):
            body(first + i * unroll + j)

    for j in range(count - count % unroll, count):
        body(first + j)


def kernel(
    T, Z, feat, tiles, trow, tcol, tcount, weight, bias, cot,
    act_out, dw_out, db_out,
    a_vm, up, dn, table, high, low, running, order_v, order, row_v, col_v, count_s,
    agg, aggs, degs, degr, aggr, nbuf, w_vm, b_vm, c_vm,
    piece, piece_in, lined, bias_line, final,
    tile_sem, row_sem, col_sem, count_sem, order_sem, w_sem, b_sem, c_sem,
    up_send, up_recv, dn_send, dn_recv, a2_send, a2_recv, g_send, g_recv, p_send, p_recv,
    n_send, n_recv, x_send, x_recv, b_send, b_recv, d_send, d_recv, e_send, e_recv,
):
    R = 2 * Z
    slots = a_vm.shape[0]
    rows = nbuf.shape[0]
    blocks = rows // SIDE
    wide = 2 * blocks
    PR = rows // T
    rem = lax.rem
    r, t = lax.axis_index("row"), lax.axis_index("team")
    k, z = lax.div(r, Z), rem(r, Z)

    def remote(src, dst, ssem, rsem, row, team):
        pltpu.make_async_remote_copy(
            src_ref=src, dst_ref=dst, send_sem=ssem, recv_sem=rsem,
            device_id={"row": row, "team": team}, device_id_type=MESH,
        ).start()

    barrier = pltpu.get_barrier_semaphore()
    S = Z // 4
    near = [*range(1, S + 1), *range(Z - S, Z)]

    def signal(row, team):
        pl.semaphore_signal(barrier, inc=1, device_id={"row": row, "team": team}, device_id_type=MESH)

    def in_plane(body):
        def both(o):
            u = rem(t + o, T)
            body(0, u)
            body(1, u)

        body(1 - k, t)
        each(T - 1, both, 1)

    for o in near:
        signal(k * Z + rem(z + o, Z), t)
    in_plane(lambda kk, u: signal(kk * Z + z, u))

    row_copy = pltpu.make_async_copy(trow, row_v, row_sem)
    col_copy = pltpu.make_async_copy(tcol, col_v, col_sem)
    count_copy = pltpu.make_async_copy(tcount, count_s, count_sem)
    row_copy.start()
    col_copy.start()
    count_copy.start()
    mine = pl.ds(pl.multiple_of(t * PR, PR), PR)
    tile_copy = pltpu.make_async_copy(tiles, a_vm, tile_sem)
    w_copy = pltpu.make_async_copy(weight, w_vm, w_sem)
    b_copy = pltpu.make_async_copy(bias, b_vm, b_sem)
    c_copy = pltpu.make_async_copy(cot, c_vm, c_sem)

    pl.semaphore_wait(barrier, len(near) + 2 * T - 1)

    ways = ((up, up_send, up_recv, 1, Z // 2), (dn, dn_send, dn_recv, -1, Z // 2 - 1))
    own_piece = feat.at[mine]
    for d in range(S, 0, -1):
        for buf, ssem, rsem, sign, far in ways:
            remote(own_piece, buf.at[d], ssem, rsem.at[d], k * Z + rem(z + sign * d + Z, Z), t)

    place = pl.ds(pl.multiple_of((k * T + t) * PR, PR), PR)

    def forward(piece_ref, source):
        remote(piece_ref, table.at[place], a2_send, a2_recv, (1 - k) * Z + z, source)

        @pl.when(source != t)
        def _():
            remote(piece_ref, table.at[place], a2_send, a2_recv, k * Z + z, source)

        @pl.when(source == t)
        def _():
            pltpu.make_async_copy(piece_ref, table.at[place], a2_recv).start()

    def relay():
        for buf, ssem, rsem, sign, far in ways:
            wait_bytes(buf.at[S], rsem.at[S])
            for e in range(far - S, 0, -1):
                remote(buf.at[S], buf.at[S + e], ssem, rsem.at[S + e], k * Z + rem(z + sign * e + Z, Z), t)

    def pass_on(distances):
        for d in distances:
            for buf, ssem, rsem, sign, far in ways:
                if d <= far:
                    if d != S:
                        wait_bytes(buf.at[d], rsem.at[d])
                    forward(buf.at[d], rem(z - sign * d + Z, Z))

    forward(own_piece, z)
    tile_copy.start()

    row_copy.wait()
    col_copy.wait()
    count_copy.wait()
    lane = lax.broadcasted_iota(jnp.int32, (slots, SIDE), 1)
    line = lax.broadcasted_iota(jnp.int32, (slots, SIDE), 0)
    owner_bits = (blocks * T).bit_length() - 1
    col = col_v[...]
    key = row_v[...] * wide + (col >> owner_bits) * blocks + (col & (blocks - 1))
    ids = lax.broadcasted_iota(jnp.int32, (1, slots), 1)
    key = jnp.where(ids < count_s[0, 0], key, SIDE - 1)
    key = jnp.broadcast_to(key, (slots, slots))
    slot = lax.broadcasted_iota(jnp.int32, (slots, slots), 1)
    here = lax.broadcasted_iota(jnp.int32, (slots, slots), 0)
    down = jnp.sum(jnp.where(slot == here, key, 0), axis=1, keepdims=True)
    ahead = (key < down) | ((key == down) & (slot < here))
    rank = jnp.sum(jnp.where(ahead, 1, 0), axis=1, keepdims=True)

    def across(mask, what):
        return jnp.sum(jnp.where(mask, what, 0), axis=0, keepdims=True)

    order_v[0:1, :] = across(rank == lane, line)
    key_at = across(rank == lane, down)
    key_before = across(rank + 1 == lane, down)
    order_v[1:2, :] = jnp.where((key_at == key_before) & (lane[0:1] > 0), 1, 0)
    population = across(down == lane, 1)
    order_v[2:3, :] = jnp.where(population > 0, across(down <= lane, 1) - 1, slots)
    order_copy = pltpu.make_async_copy(order_v, order, order_sem)
    order_copy.start()
    high[slots] = jnp.zeros((SIDE, SIDE), BF16)
    low[slots] = jnp.zeros((SIDE, SIDE), BF16)
    running[...] = jnp.zeros_like(running)
    relay()
    w_copy.start()
    b_copy.start()
    c_copy.start()
    pass_on(range(S, 0, -1))
    order_copy.wait()
    tile_copy.wait()

    chunk = 8

    def sum_tiles(c):
        held = running[...]
        for g in range(chunk):
            i = c * chunk + g
            held = jnp.where(order[1, i] > 0, held, 0.0) + a_vm[order[0, i]].astype(F32)
            top = held.astype(BF16)
            high[i] = top
            low[i] = (held - top.astype(F32)).astype(BF16)
        running[...] = held

    chunks = slots // chunk
    pl.loop(0, chunks // 2)(sum_tiles)
    pass_on(range(Z // 2, S, -1))
    pl.loop(chunks // 2, chunks)(sum_tiles)

    def dense(part, half):
        bands = []
        for b in (2 * half, 2 * half + 1):
            bands.append(jnp.concatenate([part[order[2, b * wide + c]] for c in range(wide)], axis=1))
        return jnp.concatenate(bands, axis=0)

    def product(half, right):
        got = jnp.dot(dense(high, half), right, preferred_element_type=F32)
        return got + jnp.dot(dense(low, half), right, preferred_element_type=F32)

    pair = 2 * SIDE
    across_lane = lax.broadcasted_iota(jnp.int32, (SIDE, SIDE), 1)
    down_line = lax.broadcasted_iota(jnp.int32, (SIDE, SIDE), 0)
    for half in range(blocks // 2):
        sums = product(half, jnp.ones((wide * SIDE, SIDE), BF16))
        for j in range(2):
            square = jnp.where(across_lane == down_line, sums[j * SIDE:(j + 1) * SIDE, :], 0.0)
            degs[2 * half + j] = jnp.sum(square, axis=0, keepdims=True)

    def give_degree(o):
        u = rem(t + o, T)
        remote(degs.at[lax.div(u * PR, SIDE)], degr.at[o - 1], g_send, g_recv, r, u)

    each(T - 1, give_degree, 1)
    wait_bytes(table, a2_recv)

    owners = pair // PR
    for half in range(blocks // 2):
        span = pl.ds(half * pair, pair)
        got = product(half, table[...])
        agg[span, :] = got
        aggs[span, :] = got.astype(BF16)

        def give_part(u):
            @pl.when(u != t)
            def _():
                part = pl.ds(pl.multiple_of(u * PR, PR), PR)
                remote(aggs.at[part], aggr.at[rem(u - t + T, T) - 1], p_send, p_recv, r, u)

        each(owners, give_part, half * owners)

    wait_bytes(degr, g_recv)
    degree = degs[lax.div(t * PR, SIDE)] + jnp.sum(degr[...], axis=0) + 1.0
    here = lax.broadcasted_iota(jnp.int32, (PR, SIDE), 0) + rem(t * PR, SIDE)
    here = here == lax.broadcasted_iota(jnp.int32, (PR, SIDE), 1)
    degree = jnp.sum(jnp.where(here, degree, 0.0), axis=1, keepdims=True)
    root = jnp.sqrt(degree)
    wait_bytes(aggr, p_recv)
    total = agg[mine, :]
    for o in range(T - 1):
        total += aggr[o].astype(F32)
    w_copy.wait()
    b_copy.wait()
    c_copy.wait()

    def layer(normed):
        pre = jnp.dot(normed, w_vm[...], preferred_element_type=F32) + b_vm[...]
        return pre, 1.0 / (1.0 + jnp.exp(-pre))

    normed = (total / root).astype(BF16)
    nbuf[mine, :] = normed
    pre, gate = layer(normed)
    delta = (c_vm[mine, :].astype(F32) * gate * (1.0 + pre * (1.0 - gate))).astype(BF16)
    db = jnp.sum(delta.astype(F32), axis=0, keepdims=True)
    dw = lax.dot_general(normed, delta, (((0,), (0,)), ((), ())), preferred_element_type=F32)

    SR = SIDE // T
    HR = SR // 2
    n = 2 * HR
    mine_at = k * T + t
    for q in range(2):
        for u in range(T):
            for j in range(n):
                i = u * SR + q * HR + j // 2
                piece[q * T + u, :, j * SIDE:(j + 1) * SIDE] = dw[i:i + 1, (j % 2) * SIDE:(j % 2 + 1) * SIDE]
            piece[q * T + u, :, n * SIDE:] = db[:, q * SIDE:(q + 1) * SIDE]

        def give_line(u):
            remote(piece.at[q * T + u], piece_in.at[mine_at], x_send, x_recv, q * Z + z, u)

        @pl.when(k != q)
        def _():
            give_line(t)

        each(T - 1, lambda o: give_line(rem(t + o, T)), 1)
    piece_in[mine_at] = piece[mine_at]
    rest = piece_in.at[pl.ds(0, 2 * T - 1)]
    wait_bytes(rest, x_recv)
    plane = jnp.sum(piece_in[...], axis=0)
    lined[z] = jnp.concatenate([plane[:, j * SIDE:(j + 1) * SIDE] for j in range(n)], axis=0).astype(BF16)
    bias_line[0] = plane[:, n * SIDE:]

    @pl.when(t != 0)
    def _():
        remote(bias_line.at[0], bias_line.at[1], b_send, b_recv, k * Z + rem(z + t, Z), t)

    @pl.when(t == 0)
    def _():
        bias_line[1] = plane[:, n * SIDE:]

    each(Z - 1, lambda o: remote(lined.at[z], lined.at[z], d_send, d_recv, k * Z + rem(z + o, Z), t), 1)
    each(T - 1, lambda o: remote(nbuf.at[mine], nbuf.at[mine], n_send, n_recv, r, rem(t + o, T)), 1)
    wait_bytes(lined.at[pl.ds(0, Z - 1)], d_recv)
    half_slice = jnp.sum(lined[...].astype(F32), axis=0)
    for j in range(n):
        final[mine_at, :, j * SIDE:(j + 1) * SIDE] = half_slice[j:j + 1, :]

    @pl.when(t != 0)
    def _():
        wait_bytes(bias_line.at[1], b_recv)

    final[mine_at, :, n * SIDE:] = bias_line[1]
    in_plane(lambda kk, u: remote(final.at[mine_at], final.at[mine_at], e_send, e_recv, kk * Z + z, u))

    wait_bytes(nbuf.at[pl.ds(0, (T - 1) * PR)], n_recv)
    for b in range(blocks):
        span = pl.ds(b * SIDE, SIDE)
        pre, gate = layer(nbuf[span, :])
        act_out[span, :] = (pre * gate).astype(BF16)

    wait_bytes(up.at[pl.ds(1, Z // 2)], up_send)
    wait_bytes(dn.at[pl.ds(1, Z // 2 - 1)], dn_send)
    wait_bytes(table.at[pl.ds(0, (2 * T - 1) * PR)], a2_send)
    wait_bytes(degr, g_send)
    wait_bytes(aggr, p_send)
    wait_bytes(nbuf.at[pl.ds(0, (T - 1) * PR)], n_send)
    wait_bytes(rest, x_send)

    @pl.when(t != 0)
    def _():
        wait_bytes(bias_line.at[0], b_send)

    wait_bytes(lined.at[pl.ds(0, Z - 1)], d_send)
    wait_bytes(rest, e_send)
    wait_bytes(rest, e_recv)
    for u in range(T):
        for q in range(2):
            for j in range(n):
                i = u * SR + q * HR + j // 2
                dw_out[i:i + 1, (j % 2) * SIDE:(j % 2 + 1) * SIDE] = final[q * T + u, :, j * SIDE:(j + 1) * SIDE]
    for q in range(2):
        db = final[q * T + z, :, n * SIDE:]
        for p in range(1, Z):
            db += final[q * T + rem(z - p + Z, Z), :, n * SIDE:]
        db_out[:, q * SIDE:(q + 1) * SIDE] = db


def hand_out(a, b, c, a_out, b_out, c_out, a_sem, b_sem, c_sem):
    copies = [pltpu.make_async_copy(*x) for x in ((a, a_out, a_sem), (b, b_out, b_sem), (c, c_out, c_sem))]
    for copy in copies:
        copy.start()
    for copy in copies:
        copy.wait()


def per_device(T, Z, features, tile_vals, tile_row, tile_col, tile_count, weight, bias, cotangent):
    rows, width = features.shape
    slots = tile_vals.shape[2]
    hidden = weight.shape[1]
    PR = rows // T
    SR = SIDE // T
    line = (SR + 1) * SIDE
    any_spec = pl.BlockSpec(memory_space=pl.ANY)
    vmem = pl.BlockSpec(memory_space=pltpu.VMEM)
    dma = pltpu.SemaphoreType.DMA
    V = pltpu.VMEM
    out_shape = (
        jax.ShapeDtypeStruct((rows, hidden), BF16),
        jax.ShapeDtypeStruct((width, hidden), F32),
        jax.ShapeDtypeStruct((1, hidden), F32),
    )
    results = pl.pallas_call(
        functools.partial(kernel, T, Z),
        out_shape=tuple(V(x.shape, x.dtype) for x in out_shape),
        in_specs=[any_spec] * 8,
        out_specs=(vmem,) * 3,
        scratch_shapes=[
            V((slots, SIDE, SIDE), BF16),
            V((Z // 2 + 1, PR, width), BF16),
            V((Z // 2, PR, width), BF16),
            V((2 * rows, width), BF16),
            V((slots + 1, SIDE, SIDE), BF16),
            V((slots + 1, SIDE, SIDE), BF16),
            V((SIDE, SIDE), F32),
            V((8, SIDE), jnp.int32),
            pltpu.SMEM((8, SIDE), jnp.int32),
            V((1, slots), jnp.int32),
            V((1, slots), jnp.int32),
            pltpu.SMEM((1, 1), jnp.int32),
            V((rows, width), F32),
            V((rows, width), BF16),
            V((rows // SIDE, 1, SIDE), F32),
            V((T - 1, 1, SIDE), F32),
            V((T - 1, PR, width), BF16),
            V((rows, width), BF16),
            V((width, hidden), BF16),
            V((1, hidden), F32),
            V((rows, hidden), BF16),
            V((2 * T, 1, line), F32),
            V((2 * T, 1, line), F32),
            V((Z, SR, SIDE), BF16),
            V((2, 1, SIDE), F32),
            V((2 * T, 1, line), F32),
        ]
        + [dma] * 8
        + [dma, dma((Z // 2 + 1,)), dma, dma((Z // 2 + 1,))]
        + [dma] * 16,
        compiler_params=pltpu.CompilerParams(
            collective_id=0, has_side_effects=True, vmem_limit_bytes=56 * 1024 * 1024
        ),
        cost_estimate=pl.CostEstimate(
            flops=2 * slots * SIDE * SIDE * width, bytes_accessed=2 * slots * SIDE * SIDE, transcendentals=rows * hidden
        ),
    )(
        features,
        tile_vals.reshape(slots, SIDE, SIDE),
        tile_row.reshape(1, slots),
        tile_col.reshape(1, slots),
        tile_count,
        weight,
        bias.reshape(1, hidden),
        cotangent,
    )
    activated, dw, db = pl.pallas_call(
        hand_out,
        out_shape=out_shape,
        in_specs=[vmem] * 3,
        out_specs=(any_spec,) * 3,
        scratch_shapes=[dma] * 3,
        compiler_params=pltpu.CompilerParams(vmem_limit_bytes=56 * 1024 * 1024),
    )(*(pltpu.with_memory_space_constraint(x, pltpu.VMEM) for x in results))
    return activated, dw, db.reshape(hidden)


def solution(mesh):
    in_specs = (
        P("row", None),
        P("row", "team", None, None, None),
        P("row", "team", None),
        P("row", "team", None),
        P("row", "team"),
        P(),
        P(),
        P("row", None),
    )
    out_specs = (P("row", None), P(), P())
    T = mesh.shape["team"]
    Z = mesh.shape["row"] // 2
    return jax.shard_map(
        functools.partial(per_device, T, Z), mesh=mesh, in_specs=in_specs, out_specs=out_specs, check_vma=False
    )
```

```python
import functools

import jax
import jax.numpy as jnp
from jax import lax
from jax.experimental import pallas as pl
from jax.experimental.pallas import tpu as pltpu
from jax.sharding import PartitionSpec as P

MESH = pl.DeviceIdType.MESH
BF16, F32 = jnp.bfloat16, jnp.float32
SIDE = 128


def wait_bytes(ref, sem):
    pltpu.make_async_copy(ref, ref, sem).wait()


def each(count, body, first=0):
    unroll = 5

    @pl.loop(0, count // unroll)
    def _(i):
        for j in range(unroll):
            body(first + i * unroll + j)

    for j in range(count - count % unroll, count):
        body(first + j)


def kernel(
    T, Z, feat, tiles, trow, tcol, tcount, weight, bias, cot,
    act_out, dw_out, db_out,
    a_vm, up, dn, table, high, low, running, order_v, order, row_v, col_v, count_s,
    agg, aggs, degs, degr, aggr, nbuf, w_vm, b_vm, c_vm,
    piece, piece_in, lined, bias_line, final,
    tile_sem, row_sem, col_sem, count_sem, order_sem, w_sem, b_sem, c_sem,
    up_send, up_recv, dn_send, dn_recv, a2_send, a2_recv, g_send, g_recv, p_send, p_recv,
    n_send, n_recv, x_send, x_recv, b_send, b_recv, d_send, d_recv, e_send, e_recv,
):
    R = 2 * Z
    slots = a_vm.shape[0]
    rows = nbuf.shape[0]
    blocks = rows // SIDE
    wide = 2 * blocks
    PR = rows // T
    rem = lax.rem
    r, t = lax.axis_index("row"), lax.axis_index("team")
    k, z = lax.div(r, Z), rem(r, Z)

    def remote(src, dst, ssem, rsem, row, team):
        pltpu.make_async_remote_copy(
            src_ref=src, dst_ref=dst, send_sem=ssem, recv_sem=rsem,
            device_id={"row": row, "team": team}, device_id_type=MESH,
        ).start()

    barrier = pltpu.get_barrier_semaphore()

    def signal(row, team):
        pl.semaphore_signal(barrier, inc=1, device_id={"row": row, "team": team}, device_id_type=MESH)

    def in_plane(body):
        def both(o):
            u = rem(t + o, T)
            body(0, u)
            body(1, u)

        body(1 - k, t)
        each(T - 1, both, 1)

    each(Z - 1, lambda o: signal(k * Z + rem(z + o, Z), t), 1)
    in_plane(lambda kk, u: signal(kk * Z + z, u))

    row_copy = pltpu.make_async_copy(trow, row_v, row_sem)
    col_copy = pltpu.make_async_copy(tcol, col_v, col_sem)
    count_copy = pltpu.make_async_copy(tcount, count_s, count_sem)
    row_copy.start()
    col_copy.start()
    count_copy.start()
    mine = pl.ds(pl.multiple_of(t * PR, PR), PR)
    tile_copy = pltpu.make_async_copy(tiles, a_vm, tile_sem)
    w_copy = pltpu.make_async_copy(weight, w_vm, w_sem)
    b_copy = pltpu.make_async_copy(bias, b_vm, b_sem)
    c_copy = pltpu.make_async_copy(cot, c_vm, c_sem)

    pl.semaphore_wait(barrier, Z - 1 + 2 * T - 1)

    ways = ((up, up_send, up_recv, 1, Z // 2), (dn, dn_send, dn_recv, -1, Z // 2 - 1))
    own_piece = feat.at[mine]
    for d in range(Z // 2, 0, -1):
        for buf, ssem, rsem, sign, far in ways:
            if d > far:
                continue
            remote(own_piece, buf.at[d], ssem, rsem.at[d], k * Z + rem(z + sign * d + Z, Z), t)

    place = pl.ds(pl.multiple_of((k * T + t) * PR, PR), PR)

    def forward(piece_ref, source):
        remote(piece_ref, table.at[place], a2_send, a2_recv, (1 - k) * Z + z, source)

        @pl.when(source != t)
        def _():
            remote(piece_ref, table.at[place], a2_send, a2_recv, k * Z + z, source)

        @pl.when(source == t)
        def _():
            pltpu.make_async_copy(piece_ref, table.at[place], a2_recv).start()

    def pass_on(distances):
        for d in distances:
            for buf, ssem, rsem, sign, far in ways:
                if d <= far:
                    wait_bytes(buf.at[d], rsem.at[d])
                    forward(buf.at[d], rem(z - sign * d + Z, Z))

    forward(own_piece, z)
    tile_copy.start()

    row_copy.wait()
    col_copy.wait()
    count_copy.wait()
    lane = lax.broadcasted_iota(jnp.int32, (slots, SIDE), 1)
    line = lax.broadcasted_iota(jnp.int32, (slots, SIDE), 0)
    owner_bits = (blocks * T).bit_length() - 1
    col = col_v[...]
    key = row_v[...] * wide + (col >> owner_bits) * blocks + (col & (blocks - 1))
    ids = lax.broadcasted_iota(jnp.int32, (1, slots), 1)
    key = jnp.where(ids < count_s[0, 0], key, SIDE - 1)
    key = jnp.broadcast_to(key, (slots, slots))
    slot = lax.broadcasted_iota(jnp.int32, (slots, slots), 1)
    here = lax.broadcasted_iota(jnp.int32, (slots, slots), 0)
    down = jnp.sum(jnp.where(slot == here, key, 0), axis=1, keepdims=True)
    ahead = (key < down) | ((key == down) & (slot < here))
    rank = jnp.sum(jnp.where(ahead, 1, 0), axis=1, keepdims=True)

    def across(mask, what):
        return jnp.sum(jnp.where(mask, what, 0), axis=0, keepdims=True)

    order_v[0:1, :] = across(rank == lane, line)
    key_at = across(rank == lane, down)
    key_before = across(rank + 1 == lane, down)
    order_v[1:2, :] = jnp.where((key_at == key_before) & (lane[0:1] > 0), 1, 0)
    population = across(down == lane, 1)
    order_v[2:3, :] = jnp.where(population > 0, across(down <= lane, 1) - 1, slots)
    order_copy = pltpu.make_async_copy(order_v, order, order_sem)
    order_copy.start()
    high[slots] = jnp.zeros((SIDE, SIDE), BF16)
    low[slots] = jnp.zeros((SIDE, SIDE), BF16)
    running[...] = jnp.zeros_like(running)
    pass_on(range(Z // 2, Z // 4, -1))
    w_copy.start()
    b_copy.start()
    c_copy.start()
    order_copy.wait()
    tile_copy.wait()

    chunk = 8

    def sum_tiles(c):
        held = running[...]
        for g in range(chunk):
            i = c * chunk + g
            held = jnp.where(order[1, i] > 0, held, 0.0) + a_vm[order[0, i]].astype(F32)
            top = held.astype(BF16)
            high[i] = top
            low[i] = (held - top.astype(F32)).astype(BF16)
        running[...] = held

    chunks = slots // chunk
    pl.loop(0, chunks // 2)(sum_tiles)
    pass_on(range(Z // 4, 0, -1))
    pl.loop(chunks // 2, chunks)(sum_tiles)

    def dense(part, half):
        bands = []
        for b in (2 * half, 2 * half + 1):
            bands.append(jnp.concatenate([part[order[2, b * wide + c]] for c in range(wide)], axis=1))
        return jnp.concatenate(bands, axis=0)

    def product(half, right):
        got = jnp.dot(dense(high, half), right, preferred_element_type=F32)
        return got + jnp.dot(dense(low, half), right, preferred_element_type=F32)

    pair = 2 * SIDE
    across_lane = lax.broadcasted_iota(jnp.int32, (SIDE, SIDE), 1)
    down_line = lax.broadcasted_iota(jnp.int32, (SIDE, SIDE), 0)
    for half in range(blocks // 2):
        sums = product(half, jnp.ones((wide * SIDE, SIDE), BF16))
        for j in range(2):
            square = jnp.where(across_lane == down_line, sums[j * SIDE:(j + 1) * SIDE, :], 0.0)
            degs[2 * half + j] = jnp.sum(square, axis=0, keepdims=True)

    def give_degree(o):
        u = rem(t + o, T)
        remote(degs.at[lax.div(u * PR, SIDE)], degr.at[o - 1], g_send, g_recv, r, u)

    each(T - 1, give_degree, 1)
    wait_bytes(table, a2_recv)

    owners = pair // PR
    for half in range(blocks // 2):
        span = pl.ds(half * pair, pair)
        got = product(half, table[...])
        agg[span, :] = got
        aggs[span, :] = got.astype(BF16)

        def give_part(u):
            @pl.when(u != t)
            def _():
                part = pl.ds(pl.multiple_of(u * PR, PR), PR)
                remote(aggs.at[part], aggr.at[rem(u - t + T, T) - 1], p_send, p_recv, r, u)

        each(owners, give_part, half * owners)

    wait_bytes(degr, g_recv)
    degree = degs[lax.div(t * PR, SIDE)] + jnp.sum(degr[...], axis=0) + 1.0
    here = lax.broadcasted_iota(jnp.int32, (PR, SIDE), 0) + rem(t * PR, SIDE)
    here = here == lax.broadcasted_iota(jnp.int32, (PR, SIDE), 1)
    degree = jnp.sum(jnp.where(here, degree, 0.0), axis=1, keepdims=True)
    root = jnp.sqrt(degree)
    wait_bytes(aggr, p_recv)
    total = agg[mine, :]
    for o in range(T - 1):
        total += aggr[o].astype(F32)
    w_copy.wait()
    b_copy.wait()
    c_copy.wait()

    def layer(normed):
        pre = jnp.dot(normed, w_vm[...], preferred_element_type=F32) + b_vm[...]
        return pre, 1.0 / (1.0 + jnp.exp(-pre))

    normed = (total / root).astype(BF16)
    nbuf[mine, :] = normed
    pre, gate = layer(normed)
    delta = (c_vm[mine, :].astype(F32) * gate * (1.0 + pre * (1.0 - gate))).astype(BF16)
    db = jnp.sum(delta.astype(F32), axis=0, keepdims=True)
    dw = lax.dot_general(normed, delta, (((0,), (0,)), ((), ())), preferred_element_type=F32)

    SR = SIDE // T
    HR = SR // 2
    n = 2 * HR
    mine_at = k * T + t
    for q in range(2):
        for u in range(T):
            for j in range(n):
                i = u * SR + q * HR + j // 2
                piece[q * T + u, :, j * SIDE:(j + 1) * SIDE] = dw[i:i + 1, (j % 2) * SIDE:(j % 2 + 1) * SIDE]
            piece[q * T + u, :, n * SIDE:] = db[:, q * SIDE:(q + 1) * SIDE]

        def give_line(u):
            remote(piece.at[q * T + u], piece_in.at[mine_at], x_send, x_recv, q * Z + z, u)

        @pl.when(k != q)
        def _():
            give_line(t)

        each(T - 1, lambda o: give_line(rem(t + o, T)), 1)
    piece_in[mine_at] = piece[mine_at]
    rest = piece_in.at[pl.ds(0, 2 * T - 1)]
    wait_bytes(rest, x_recv)
    plane = jnp.sum(piece_in[...], axis=0)
    lined[z] = jnp.concatenate([plane[:, j * SIDE:(j + 1) * SIDE] for j in range(n)], axis=0).astype(BF16)
    bias_line[0] = plane[:, n * SIDE:]

    @pl.when(t != 0)
    def _():
        remote(bias_line.at[0], bias_line.at[1], b_send, b_recv, k * Z + rem(z + t, Z), t)

    @pl.when(t == 0)
    def _():
        bias_line[1] = plane[:, n * SIDE:]

    each(Z - 1, lambda o: remote(lined.at[z], lined.at[z], d_send, d_recv, k * Z + rem(z + o, Z), t), 1)
    each(T - 1, lambda o: remote(nbuf.at[mine], nbuf.at[mine], n_send, n_recv, r, rem(t + o, T)), 1)
    wait_bytes(lined.at[pl.ds(0, Z - 1)], d_recv)
    half_slice = jnp.sum(lined[...].astype(F32), axis=0)
    for j in range(n):
        final[mine_at, :, j * SIDE:(j + 1) * SIDE] = half_slice[j:j + 1, :]

    @pl.when(t != 0)
    def _():
        wait_bytes(bias_line.at[1], b_recv)

    final[mine_at, :, n * SIDE:] = bias_line[1]
    in_plane(lambda kk, u: remote(final.at[mine_at], final.at[mine_at], e_send, e_recv, kk * Z + z, u))

    wait_bytes(nbuf.at[pl.ds(0, (T - 1) * PR)], n_recv)
    for b in range(blocks):
        span = pl.ds(b * SIDE, SIDE)
        pre, gate = layer(nbuf[span, :])
        act_out[span, :] = (pre * gate).astype(BF16)

    wait_bytes(up.at[pl.ds(1, Z // 2)], up_send)
    wait_bytes(dn.at[pl.ds(1, Z // 2 - 1)], dn_send)
    wait_bytes(table.at[pl.ds(0, (2 * T - 1) * PR)], a2_send)
    wait_bytes(degr, g_send)
    wait_bytes(aggr, p_send)
    wait_bytes(nbuf.at[pl.ds(0, (T - 1) * PR)], n_send)
    wait_bytes(rest, x_send)

    @pl.when(t != 0)
    def _():
        wait_bytes(bias_line.at[0], b_send)

    wait_bytes(lined.at[pl.ds(0, Z - 1)], d_send)
    wait_bytes(rest, e_send)
    wait_bytes(rest, e_recv)
    for u in range(T):
        for q in range(2):
            for j in range(n):
                i = u * SR + q * HR + j // 2
                dw_out[i:i + 1, (j % 2) * SIDE:(j % 2 + 1) * SIDE] = final[q * T + u, :, j * SIDE:(j + 1) * SIDE]
    for q in range(2):
        db = final[q * T + z, :, n * SIDE:]
        for p in range(1, Z):
            db += final[q * T + rem(z - p + Z, Z), :, n * SIDE:]
        db_out[:, q * SIDE:(q + 1) * SIDE] = db


def hand_out(a, b, c, a_out, b_out, c_out, a_sem, b_sem, c_sem):
    copies = [pltpu.make_async_copy(*x) for x in ((a, a_out, a_sem), (b, b_out, b_sem), (c, c_out, c_sem))]
    for copy in copies:
        copy.start()
    for copy in copies:
        copy.wait()


def per_device(T, Z, features, tile_vals, tile_row, tile_col, tile_count, weight, bias, cotangent):
    rows, width = features.shape
    slots = tile_vals.shape[2]
    hidden = weight.shape[1]
    PR = rows // T
    SR = SIDE // T
    line = (SR + 1) * SIDE
    any_spec = pl.BlockSpec(memory_space=pl.ANY)
    vmem = pl.BlockSpec(memory_space=pltpu.VMEM)
    dma = pltpu.SemaphoreType.DMA
    V = pltpu.VMEM
    out_shape = (
        jax.ShapeDtypeStruct((rows, hidden), BF16),
        jax.ShapeDtypeStruct((width, hidden), F32),
        jax.ShapeDtypeStruct((1, hidden), F32),
    )
    results = pl.pallas_call(
        functools.partial(kernel, T, Z),
        out_shape=tuple(V(x.shape, x.dtype) for x in out_shape),
        in_specs=[any_spec] * 8,
        out_specs=(vmem,) * 3,
        scratch_shapes=[
            V((slots, SIDE, SIDE), BF16),
            V((Z // 2 + 1, PR, width), BF16),
            V((Z // 2, PR, width), BF16),
            V((2 * rows, width), BF16),
            V((slots + 1, SIDE, SIDE), BF16),
            V((slots + 1, SIDE, SIDE), BF16),
            V((SIDE, SIDE), F32),
            V((8, SIDE), jnp.int32),
            pltpu.SMEM((8, SIDE), jnp.int32),
            V((1, slots), jnp.int32),
            V((1, slots), jnp.int32),
            pltpu.SMEM((1, 1), jnp.int32),
            V((rows, width), F32),
            V((rows, width), BF16),
            V((rows // SIDE, 1, SIDE), F32),
            V((T - 1, 1, SIDE), F32),
            V((T - 1, PR, width), BF16),
            V((rows, width), BF16),
            V((width, hidden), BF16),
            V((1, hidden), F32),
            V((rows, hidden), BF16),
            V((2 * T, 1, line), F32),
            V((2 * T, 1, line), F32),
            V((Z, SR, SIDE), BF16),
            V((2, 1, SIDE), F32),
            V((2 * T, 1, line), F32),
        ]
        + [dma] * 8
        + [dma, dma((Z // 2 + 1,)), dma, dma((Z // 2 + 1,))]
        + [dma] * 16,
        compiler_params=pltpu.CompilerParams(
            collective_id=0, has_side_effects=True, vmem_limit_bytes=56 * 1024 * 1024
        ),
        cost_estimate=pl.CostEstimate(
            flops=2 * slots * SIDE * SIDE * width, bytes_accessed=2 * slots * SIDE * SIDE, transcendentals=rows * hidden
        ),
    )(
        features,
        tile_vals.reshape(slots, SIDE, SIDE),
        tile_row.reshape(1, slots),
        tile_col.reshape(1, slots),
        tile_count,
        weight,
        bias.reshape(1, hidden),
        cotangent,
    )
    activated, dw, db = pl.pallas_call(
        hand_out,
        out_shape=out_shape,
        in_specs=[vmem] * 3,
        out_specs=(any_spec,) * 3,
        scratch_shapes=[dma] * 3,
        compiler_params=pltpu.CompilerParams(vmem_limit_bytes=56 * 1024 * 1024),
    )(*(pltpu.with_memory_space_constraint(x, pltpu.VMEM) for x in results))
    return activated, dw, db.reshape(hidden)


def solution(mesh):
    in_specs = (
        P("row", None),
        P("row", "team", None, None, None),
        P("row", "team", None),
        P("row", "team", None),
        P("row", "team"),
        P(),
        P(),
        P("row", None),
    )
    out_specs = (P("row", None), P(), P())
    T = mesh.shape["team"]
    Z = mesh.shape["row"] // 2
    return jax.shard_map(
        functools.partial(per_device, T, Z), mesh=mesh, in_specs=in_specs, out_specs=out_specs, check_vma=False
    )
```
